256 devices in a mesh: dp: 64 (over z, y, core), mp: 4 (over x).
Axes of the slice: x: 4, y: 4, z: 8, core: 2. Of those that a mesh axis runs over, the one named last changes fastest.
Arguments:
- query_rows: bfloat16 [16384, 6144], P(('dp', 'mp')), may hold values from -6 to 6
- key_rows: bfloat16 [16384, 6144], P(('dp', 'mp')), may hold values from -6 to 6
- value_rows: bfloat16 [16384, 6144], P(('dp', 'mp')), may hold values from -6 to 6
- destination: int32 [16384], replicated, may hold values from 0 to 63, as said below
- image_slot: int32 [16384], replicated, may hold values from 0 to 5
- gain_query: float32 [48, 128], P('mp'), may hold values from 0.5 to 5
- gain_key: float32 [48, 128], P('mp'), may hold values from 0.5 to 5
- grad_output: bfloat16 [32768, 6144], P('dp', 'mp'), may hold values from -16 to 16
Outputs:
- attention_out: bfloat16 [16384, 6144], P(('dp', 'mp'))
- grad_query: bfloat16 [16384, 6144], P(('dp', 'mp'))
- grad_key: bfloat16 [16384, 6144], P(('dp', 'mp'))
- grad_value: bfloat16 [16384, 6144], P(('dp', 'mp'))
- grad_gain_query: float32 [48, 128], P('mp', 'dp')
- grad_gain_key: float32 [48, 128], P('mp', 'dp')
The draws below stay inside these ranges and needn't reach their ends.
Inputs may be any that keep to these rules, and one draw needn't show every extreme that they name: `destination`: each loader row's data group. Among the rows of one loader device no group is named more than 2 times, and in every draw some group is named exactly 2 times by the rows of every loader device.
All inputs are finite; a program needn't handle non-finite values.
Results may differ from the reference program's by a relative error of at most 0.005.
The reference program's roundings to bfloat16 on the way count: a program that leaves them out, or rounds other values in their place, can miss the bound.
Values may be sent and summed in bfloat16 or wider, within the bound.
A program may use at most 128 MiB of HBM per device.

```python
import math
import jax
import jax.numpy as jnp
from jax import lax

HEADS = 48
HD = 128
LOAD_ROWS = 64
IMGS = 6
CAP = 2
SLOTS = 512
ROWS_ALL = 16384
GROUP_ROWS = 32768
N_DP = 64
N_MP = 4


def shared_rows(key):
    return jnp.clip(jax.random.normal(key, (ROWS_ALL, HEADS * HD), jnp.float32), -6.0, 6.0)


def draw_query_rows(key, part):
    shared_base = shared_rows(key)
    return shared_base.astype(jnp.bfloat16)


def draw_key_rows(key, part):
    key = jax.random.fold_in(key, 5)
    independent = jnp.clip(jax.random.normal(jax.random.fold_in(key, 1), (ROWS_ALL, HEADS * HD), jnp.float32), -6.0, 6.0)
    return independent.astype(jnp.bfloat16)


def draw_destination(key, part):
    key = jax.random.fold_in(key, 11)
    sources = N_DP * N_MP
    slot_total = N_DP * CAP
    busiest = jax.random.randint(jax.random.fold_in(key, 1), (), 0, N_DP)
    source_keys = jax.random.split(jax.random.fold_in(key, 2), sources)
    slot_group = jnp.arange(slot_total, dtype=jnp.int32) // CAP

    def one_source(source_key):
        first_key, second_key = jax.random.split(source_key)
        priority_order = jax.random.permutation(first_key, slot_total).astype(jnp.int32)
        priority = jnp.where(slot_group == busiest, priority_order - slot_total, priority_order)
        chosen = jnp.argsort(priority)[:LOAD_ROWS]
        chosen_groups = (chosen // CAP).astype(jnp.int32)
        return chosen_groups[jax.random.permutation(second_key, LOAD_ROWS)]
    return jax.vmap(one_source)(source_keys).reshape(-1).astype(jnp.int32)


def gain_table(key, lower, upper):
    return jnp.exp(jax.random.uniform(key, (HEADS, HD), jnp.float32, minval=lower, maxval=upper))


def draw_gain_query(key, part):
    key = jax.random.fold_in(key, 7)
    return gain_table(key, -0.6931, 0.6931)


def draw_gain_key(key, part):
    key = jax.random.fold_in(key, 9)
    return gain_table(key, -0.6931, 0.6931)


def draw_grad_output(key, part):
    key = jax.random.fold_in(key, 13)
    group_of_row = (jnp.arange(GROUP_ROWS) // SLOTS).astype(jnp.float32)
    rising = 1.0 + 2.0 * group_of_row / max(N_DP - 1, 1)
    noise = jnp.clip(jax.random.normal(jax.random.fold_in(key, 1), (GROUP_ROWS, HEADS * HD), jnp.float32), -6.0, 6.0)
    return jnp.clip(noise * rising[:, None], -16.0, 16.0).astype(jnp.bfloat16)


def plant(drawn, rng, least, high):
    shape = drawn.shape
    spot = [jax.random.randint(jax.random.fold_in(rng, axis), (), 0, shape[axis]) for axis in range(len(shape))]
    drawn = drawn.at[tuple(spot)].set(least)
    longest = shape.index(max(shape))
    spot[longest] = (spot[longest] + 1) % shape[longest]
    return drawn.at[tuple(spot)].set(high)


def levels(stream_key, shape, cuts, low, high):
    factor_of = 1.0
    for dim, blocks in cuts:
        heights = jax.random.uniform(jax.random.fold_in(jax.random.fold_in(stream_key, 6), dim), (blocks,), jnp.float32, low / len(cuts), high / len(cuts))
        factor_of = factor_of * jnp.repeat(jnp.exp(heights), shape[dim] // blocks).reshape((-1,) + (1,) * (len(shape) - 1 - dim))
    return factor_of


def normal_values(key, shape, width, bound, shards=(), held_as=jnp.bfloat16):
    result = width * jax.random.normal(key, shape, jnp.float32)
    if shards:
        result = result * levels(key, shape, shards, -0.22, 0.18)
    return jnp.clip(result, -bound, bound).astype(held_as)


def setup_inputs(seed: int = 0) -> dict:
    streams_of = jax.random.split(jax.random.key(seed), 9)
    return {
        "query_rows": draw_query_rows(jax.random.fold_in(streams_of[8], 71), 0),
        "key_rows": draw_key_rows(jax.random.fold_in(streams_of[8], 71), 0),
        "value_rows": normal_values(streams_of[2], (ROWS_ALL, HEADS * HD), 1.0, 6.0, ((0, 256),)),
        "destination": draw_destination(jax.random.fold_in(streams_of[8], 71), 0),
        "image_slot": plant(jax.random.randint(streams_of[4], (ROWS_ALL,), 0, IMGS), jax.random.fold_in(streams_of[4], 1), 0, IMGS - 1).astype(jnp.int32),
        "gain_query": draw_gain_query(jax.random.fold_in(streams_of[8], 71), 0),
        "gain_key": draw_gain_key(jax.random.fold_in(streams_of[8], 71), 0),
        "grad_output": draw_grad_output(jax.random.fold_in(streams_of[8], 71), 0),
    }


EPSILON = 1e-06

def normalize(block):
    floats = block.astype(jnp.float32)
    average = lax.optimization_barrier(jnp.mean(floats, axis=-1, keepdims=True))
    centred = floats - average
    inverse = lax.rsqrt(lax.optimization_barrier(jnp.mean(centred * centred, axis=-1, keepdims=True)) + EPSILON)
    return (centred * inverse, inverse)

def norm_back(grad_hat, normed, inverse):
    first = lax.optimization_barrier(jnp.mean(grad_hat, axis=-1, keepdims=True))
    second = lax.optimization_barrier(jnp.mean(grad_hat * normed, axis=-1, keepdims=True))
    return inverse * (grad_hat - first - normed * second)

def head_pass(query_head, key_head, value_head, grad_head, gain_for_query, gain_for_key, allowed):
    query_hat, query_inverse = normalize(query_head)
    key_hat, key_inverse = normalize(key_head)
    query_low = (query_hat * gain_for_query).astype(jnp.bfloat16)
    key_low = (key_hat * gain_for_key).astype(jnp.bfloat16)
    score_scale = 1.0 / math.sqrt(query_head.shape[-1])
    scores = jnp.dot(query_low, key_low.T, preferred_element_type=jnp.float32) * score_scale
    scores = jnp.where(allowed, scores, -1e+30)
    row_max = lax.optimization_barrier(jnp.max(scores, axis=-1, keepdims=True))
    weights = jnp.where(allowed, jnp.exp(scores - row_max), 0.0)
    attention = weights / lax.optimization_barrier(jnp.sum(weights, axis=-1, keepdims=True))
    attn_low = attention.astype(jnp.bfloat16)
    attn_out = jnp.dot(attn_low, value_head, preferred_element_type=jnp.float32).astype(jnp.bfloat16)
    grad_probs = jnp.dot(grad_head, value_head.T, preferred_element_type=jnp.float32)
    grad_value = jnp.dot(attn_low.T, grad_head, preferred_element_type=jnp.float32).astype(jnp.bfloat16)
    row_dot = lax.optimization_barrier(jnp.sum(attention * grad_probs, axis=-1, keepdims=True))
    grad_scores = (attention * (grad_probs - row_dot) * score_scale).astype(jnp.bfloat16)
    grad_qnorm = jnp.dot(grad_scores, key_low, preferred_element_type=jnp.float32)
    grad_knorm = jnp.dot(grad_scores.T, query_low, preferred_element_type=jnp.float32)
    query_term = lax.optimization_barrier(jnp.sum(grad_qnorm * query_hat, axis=0))
    key_term = lax.optimization_barrier(jnp.sum(grad_knorm * key_hat, axis=0))
    grad_query = norm_back(grad_qnorm * gain_for_query, query_hat, query_inverse).astype(jnp.bfloat16)
    grad_key = norm_back(grad_knorm * gain_for_key, key_hat, key_inverse).astype(jnp.bfloat16)
    return (attn_out, grad_query, grad_key, grad_value, query_term, key_term)

def slot_table(destination, image_slot, group_id):
    sources = N_DP * N_MP
    member = destination.reshape(sources, LOAD_ROWS) == group_id
    row_rank = jnp.cumsum(member.astype(jnp.int32), axis=1) - 1
    matches = member[:, None, :] & (row_rank[:, None, :] == jnp.arange(CAP, dtype=jnp.int32)[None, :, None])
    occupied = jnp.any(matches, axis=-1)
    row_index = lax.optimization_barrier(jnp.sum(jnp.where(matches, jnp.arange(LOAD_ROWS, dtype=jnp.int32)[None, None, :], 0), axis=-1))
    anchor = (jnp.arange(sources, dtype=jnp.int32)[:, None] * LOAD_ROWS + row_index).astype(jnp.int32)
    image_of = lax.optimization_barrier(jnp.sum(jnp.where(matches, image_slot.reshape(sources, LOAD_ROWS)[:, None, :], 0), axis=-1))

    def arrange(label_table):
        return label_table.reshape(N_DP, N_MP, CAP).transpose(1, 0, 2).reshape(-1)
    return (arrange(anchor), arrange(occupied), arrange(image_of))

def reference(query_rows, key_rows, value_rows, destination, image_slot, gain_query, gain_key, grad_output):
    features = HEADS * HD
    blank = jnp.zeros((ROWS_ALL, features), jnp.bfloat16)
    gain_zero = jnp.zeros((HEADS, HD), jnp.float32)

    def one_group(group_id, carry):
        group_id = group_id.astype(jnp.int32)
        anchor, occupied, image_of = slot_table(destination, image_slot, group_id)
        target = jnp.where(occupied, anchor, ROWS_ALL).astype(jnp.int32)

        def fetch(source_rows):
            placed = jnp.take(source_rows, anchor, axis=0)
            placed = jnp.where(occupied[:, None], placed, jnp.zeros((), jnp.bfloat16))
            return placed.reshape(SLOTS, HEADS, HD).transpose(1, 0, 2)
        grad_block = lax.dynamic_slice_in_dim(grad_output, (group_id * SLOTS).astype(jnp.int32), SLOTS, 0)
        cotangent = jnp.where(occupied[:, None], grad_block, jnp.zeros((), jnp.bfloat16))
        cotangent = cotangent.reshape(SLOTS, HEADS, HD).transpose(1, 0, 2)
        same_image = image_of[:, None] == image_of[None, :]
        filled_pair = occupied[:, None] & occupied[None, :]
        diagonal_mask = jnp.arange(SLOTS)[:, None] == jnp.arange(SLOTS)[None, :]
        allowed = filled_pair & same_image | diagonal_mask
        results = lax.map(lambda bundle: head_pass(*bundle, allowed), (fetch(query_rows), fetch(key_rows), fetch(value_rows), cotangent, gain_query, gain_key))
        updated = tuple((carry[place].at[target].set(results[place].transpose(1, 0, 2).reshape(SLOTS, features), mode='drop') for place in range(4)))
        return updated + (carry[4] + results[4], carry[5] + results[5])
    final = lax.fori_loop(0, N_DP, one_group, (blank, blank, blank, blank, gain_zero, gain_zero))
    return (final[0], final[1], final[2], final[3], final[4], final[5])
```

```python
import functools
import math

import jax
import jax.numpy as jnp
from jax import lax
from jax.experimental import pallas as pl
from jax.experimental.pallas import tpu as pltpu
from jax.sharding import PartitionSpec as P

NZ, NY, NC, NX = 8, 4, 2, 4
POOL = NY * NX
ROWS = 64
WIDE = POOL * ROWS
HD = 128
NH = 3
SLOTS = 512
HALF = SLOTS // NC
PART = HALF // NZ
FEATURES = 6144
EPSILON = 1e-06
MESH = pl.DeviceIdType.MESH
BF = jnp.bfloat16
F32 = jnp.float32
VMEM_LIMIT = 60 * 1024 * 1024


def iota(shape, dim):
    return lax.broadcasted_iota(jnp.int32, shape, dim)


def dot(a, b, ca=1, cb=0):
    return lax.dot_general(a, b, (((ca,), (cb,)), ((), ())), preferred_element_type=F32)


def onehot(flags):
    return jnp.where(flags, 1.0, 0.0).astype(BF)


def coords():
    dp = lax.axis_index("dp")
    return (lax.div(dp, 8), lax.rem(lax.div(dp, 2), 4), lax.rem(dp, 2), lax.axis_index("mp"))


def device(z, y, c, x):
    return ((z * NY + y) * NC + c, x)


def build_tables(cap, z, c, codes, place, expand, lab_col, lab_row, tri):
    lane = iota((1, WIDE), 1)
    lower, upper = iota((WIDE, WIDE), 0), iota((WIDE, WIDE), 1)
    earlier = lower < upper
    tri[...] = onehot(earlier)
    own = codes[pl.ds(z * NC + c, 1), :]
    own_plane = own >> 6
    planes = own_plane == iota((NZ, WIDE), 0)
    mine = jnp.concatenate([codes[pl.ds(u * NC + c, 1), :] for u in range(NZ)], axis=0)
    members = (mine >> 6) == z
    both = jnp.concatenate([onehot(planes), onehot(members)], axis=0)
    before = dot(both, tri[...])
    own_rank = jnp.sum(jnp.where(planes, before[:NZ], 0.0), axis=0, keepdims=True)
    position = own_rank.astype(jnp.int32) + own_plane * cap
    for step in range(NZ):
        place[pl.ds(step * cap, cap), :] = onehot(position == iota((cap, WIDE), 0) + step * cap)
    message_rank = jnp.where(members, before[NZ:], -1.0).astype(jnp.int32)
    tri[...] = onehot(earlier & ((lower >> 6) == (upper >> 6)))
    order = [(jj, cc) for cc in range(NC) for jj in range(NY)]
    source = (lane >> 6) * 2
    for u in range(NZ):
        for k in range(NC):
            core = c if k == 0 else 1 - c
            row = codes[pl.ds(u * NC + core, 1), :]
            group = iota((NZ, WIDE), 0)
            name = z * 8 + (group & 3) * 2 + jnp.where(group < NY, c, 1 - c)
            member = (row >> 3) == name
            count = dot(onehot(member), tri[...])
            slot = jnp.where(member, count + source.astype(F32), -1.0)
            groups = NZ if k == 0 else NY
            blocks = [slot[g : g + 1, :].astype(jnp.int32) == iota((PART, WIDE), 0) for g in range(groups)]
            chosen = onehot(jnp.concatenate(blocks, axis=0))
            image = jnp.broadcast_to(((row & 7) + 1).astype(F32), (HD, WIDE)).astype(BF)
            label = dot(chosen[: NY * PART], image, 1, 1)
            for g in range(NY):
                at = pl.multiple_of(core * HALF + u * PART, PART)
                found = label[g * PART : (g + 1) * PART]
                empty = -1.0 - (at + iota((PART, HD), 0)).astype(F32)
                lab_col[g, pl.ds(at, PART), :] = jnp.where(found > 0.5, found, empty)
            if k == 0:
                ranks = onehot(message_rank[u : u + 1, :] == iota((cap, WIDE), 0))
                expand[u] = dot(chosen, ranks, 1, 1).astype(BF)
    for g in range(NY):
        lab_row[g] = lab_col[g].T[:8]


def normalize(block):
    floats = block.astype(F32)
    average = jnp.mean(floats, axis=-1, keepdims=True)
    centred = floats - average
    inverse = lax.rsqrt(jnp.mean(centred * centred, axis=-1, keepdims=True) + EPSILON)
    return centred * inverse, inverse


def norm_back(grad_hat, normed, inverse):
    first = jnp.mean(grad_hat, axis=-1, keepdims=True)
    second = jnp.mean(grad_hat * normed, axis=-1, keepdims=True)
    return inverse * (grad_hat - first - normed * second)


def head_pass(query, key, value, cot, gain_q, gain_k, col, row, width=256):
    scale = 1.0 / math.sqrt(HD)
    query_hat, query_inverse = normalize(query)
    key_hat, key_inverse = normalize(key)
    query_low = (query_hat * gain_q).astype(BF)
    key_low = (key_hat * gain_k).astype(BF)
    col = jnp.concatenate([col] * (width // HD), axis=1)
    outs, grads_q = [], []
    grad_v = jnp.zeros((SLOTS, HD), F32)
    grad_k = jnp.zeros((SLOTS, HD), F32)
    for at in range(0, SLOTS, width):
        q = query_low[at : at + width]
        g = cot[at : at + width]
        scores = dot(key_low, q, 1, 1)
        scores = jnp.where(col == row[:, at : at + width], scores, -1e30)
        top = jnp.max(scores, axis=0, keepdims=True)
        weights = jnp.exp((scores - top) * scale)
        attention = weights * (1.0 / jnp.sum(weights, axis=0, keepdims=True))
        low = attention.astype(BF)
        probs = dot(value, g, 1, 1)
        inner = jnp.sum(attention * probs, axis=0, keepdims=True)
        grad_s = (attention * (probs - inner) * scale).astype(BF)
        outs.append(dot(low, value, 0, 0))
        grads_q.append(dot(grad_s, key_low, 0, 0))
        grad_v = grad_v + dot(low, g)
        grad_k = grad_k + dot(grad_s, q)
    grad_q = jnp.concatenate(grads_q, axis=0)
    term_q = jnp.sum(grad_q * query_hat, axis=0, keepdims=True)
    term_k = jnp.sum(grad_k * key_hat, axis=0, keepdims=True)
    back_q = norm_back(grad_q * gain_q, query_hat, query_inverse)
    back_k = norm_back(grad_k * gain_k, key_hat, key_inverse)
    packed = jnp.concatenate(
        [jnp.concatenate(outs, axis=0).astype(BF), back_q.astype(BF), back_k.astype(BF), grad_v.astype(BF)],
        axis=1,
    )
    return packed, term_q, term_k


def main_kernel(
    cap, query_in, key_in, value_in, grad_in, gain_q, gain_k, codes, out, gain_out,
    rows, grads, xin, gob, zout, zin, half_out, packed, res, rin, zro, zri,
    place, expand, lab_col, lab_row, tri, shuffle, gacc, gz, gs, gm, gt, gy,
    load_sem, own_sem, grad_own, out_own, xs, xr, gos, gor, zs, zr, hs, hr, rs, rr, zrs, zrr, us, ur,
    gzs, gzr, gms, gmr, gys, gyr,
):
    uout = xin
    z, y, c, x = coords()
    spot = y * NX + x
    loads = [
        pltpu.make_async_copy(ref, rows.at[k], load_sem.at[k])
        for k, ref in enumerate((query_in, key_in, value_in))
    ]
    loads.append(pltpu.make_async_copy(grad_in, grads, load_sem.at[3]))
    for load in loads:
        load.start()

    barrier = pltpu.get_barrier_semaphore()

    def greet(target):
        pl.semaphore_signal(barrier, inc=1, device_id=target, device_id_type=MESH)

    def xy_peer(i):
        return lax.rem(y + lax.div(i, NX), NY), lax.rem(x + lax.rem(i, NX), NX)

    def xy_source(i):
        return lax.rem(y + NY - lax.div(i, NX), NY), lax.rem(x + NX - lax.rem(i, NX), NX)

    def each(low, high, body):
        def step(i, carry):
            body(i)
            return carry

        lax.fori_loop(low, high, step, 0)

    def greet_xy(i):
        py, px = xy_peer(i)
        greet(device(z, py, c, px))

    def greet_z(d):
        greet(device(lax.rem(z + d, NZ), y, c, x))

    each(1, POOL, greet_xy)
    each(1, NZ, greet_z)
    mate = device(z, y, 1 - c, x)
    greet(mate)
    pl.semaphore_wait(barrier, POOL - 1 + NZ - 1 + 1)

    def remote(src, dst, send, recv, target):
        return pltpu.make_async_remote_copy(
            src_ref=src, dst_ref=dst, send_sem=send, recv_sem=recv, device_id=target, device_id_type=MESH
        )

    def columns(py, px, h):
        return pl.ds(pl.multiple_of(px * 1536 + py * 384 + h * HD, HD), HD)

    def xy_copy(h, i):
        py, px = xy_peer(i)
        return remote(
            rows.at[:, :, columns(py, px, h)], xin.at[h, 0:3, spot], xs.at[h, i], xr.at[h, i], device(z, py, c, px)
        )

    def xy_arrival(h, i):
        py, px = xy_source(i)
        return remote(
            rows.at[:, :, columns(y, x, h)], xin.at[h, 0:3, py * NX + px], xs.at[h, i], xr.at[h, i], device(z, py, c, px)
        )

    def xy_own(h):
        return pltpu.make_async_copy(rows.at[:, :, columns(y, x, h)], xin.at[h, 0:3, spot], own_sem.at[h])

    def grad_columns(py, h):
        return pl.ds(pl.multiple_of(py * 384 + h * HD, HD), HD)

    def grad_copy(h, d):
        py = lax.rem(y + d, NY)
        return remote(grads.at[:, grad_columns(py, h)], gob.at[h, y], gos.at[h, d], gor.at[h, d], device(z, py, c, x))

    def grad_arrival(h, d):
        py = lax.rem(y + NY - d, NY)
        return remote(grads.at[:, grad_columns(y, h)], gob.at[h, py], gos.at[h, d], gor.at[h, d], device(z, py, c, x))

    def grad_keep(h):
        return pltpu.make_async_copy(grads.at[:, grad_columns(y, h)], gob.at[h, y], grad_own.at[h])

    for load in loads:
        load.wait()

    def send_rows(h):
        each(1, POOL, lambda i: xy_copy(h, i).start())
        xy_own(h).start()
        each(1, NY, lambda d: grad_copy(h, d).start())
        grad_keep(h).start()

    each(0, NH, send_rows)

    build_tables(cap, z, c, codes, place, expand, lab_col, lab_row, tri)
    slot = iota((SLOTS, SLOTS), 0)
    pool = (slot >> 1) & 15
    canon = (pool & 3) * 128 + ((slot >> 5) & 7) * 16 + (pool >> 2) * 4 + (slot >> 8) * 2 + (slot & 1)
    shuffle[...] = onehot(canon == iota((SLOTS, SLOTS), 1))
    gacc[...] = jnp.zeros_like(gacc)

    def z_copy(h, d):
        pz = lax.rem(z + d, NZ)
        return remote(zout.at[h, pz], zin.at[h, z], zs.at[h, d], zr.at[h, d], device(pz, y, c, x))

    def z_arrival(h, d):
        pz = lax.rem(z + NZ - d, NZ)
        return remote(zout.at[h, pz], zin.at[h, pz], zs.at[h, d], zr.at[h, d], device(pz, y, c, x))

    def message(h, pz):
        pooled = jnp.concatenate([xin[h, k].reshape(WIDE, HD) for k in range(3)], axis=1)
        chosen = place[pl.ds(pl.multiple_of(pz * cap, 16), cap), :]
        return dot(chosen, pooled).astype(BF)

    def compact(h):
        each(1, POOL, lambda i: xy_arrival(h, i).wait_recv())
        xy_own(h).wait()

        def to_plane(d):
            pz = lax.rem(z + d, NZ)
            zout[h, pz] = message(h, pz)
            z_copy(h, d).start()

        each(1, NZ, to_plane)
        zin[h, z] = message(h, z)

    each(0, NH, compact)

    def half_copy(h):
        return remote(half_out.at[h], packed.at[h, :, c], hs.at[h], hr.at[h], mate)

    def half_arrival(h):
        return remote(half_out.at[h], packed.at[h, :, 1 - c], hs.at[h], hr.at[h], mate)

    def res_copy(h):
        return remote(res.at[h, 1 - c], rin.at[h], rs.at[h], rr.at[h], mate)

    def back_copy(h, d):
        pz = lax.rem(z + d, NZ)
        return remote(zro.at[h, pz], zri.at[h, z], zrs.at[h, d], zrr.at[h, d], device(pz, y, c, x))

    def back_arrival(h, d):
        pz = lax.rem(z + NZ - d, NZ)
        return remote(zro.at[h, pz], zri.at[h, pz], zrs.at[h, d], zrr.at[h, d], device(pz, y, c, x))

    def work(h):
        def unfold(pz):
            spread = dot(expand[pz], zin[h, pz]).astype(BF)
            at = pl.ds(pl.multiple_of(pz * PART, PART), PART)
            for g in range(NY):
                packed[h, g, c, at, :] = spread[g * PART : (g + 1) * PART]
                half_out[h, g, at, :] = spread[(NY + g) * PART : (NY + g + 1) * PART]

        unfold(z)

        def arrive(d):
            z_arrival(h, d).wait_recv()
            unfold(lax.rem(z + NZ - d, NZ))

        each(1, NZ, arrive)
        half_copy(h).start()
        each(1, NY, lambda d: grad_arrival(h, d).wait_recv())
        grad_keep(h).wait()
        half_arrival(h).wait_recv()

        head = y * NH + h
        own_gain_q = gain_q[pl.ds(head, 1), :]
        own_gain_k = gain_k[pl.ds(head, 1), :]

        def group(g):
            block = packed[h, g].reshape(SLOTS, 3 * HD)
            col = lab_col[g]
            cot = dot(shuffle[...], gob[h, g])
            cot = jnp.where(col > 0.0, cot, 0.0).astype(BF)
            result, term_q, term_k = head_pass(
                block[:, :HD], block[:, HD : 2 * HD], block[:, 2 * HD :], cot,
                own_gain_q, own_gain_k, col, lab_row[g, 0:1, :],
            )
            res[h, 0, g] = result[:HALF]
            res[h, 1, g] = result[HALF:]
            gacc[h, 0:1, :] += term_q
            gacc[h, 1:2, :] += term_k

        each(0, NY, group)
        res_copy(h).start()
        res_copy(h).wait_recv()

        def fold(pz):
            at = pl.ds(pl.multiple_of(pz * PART, PART), PART)
            blocks = [res[h, c, g, at, :] for g in range(NY)] + [rin[h, g, at, :] for g in range(NY)]
            return dot(expand[pz], jnp.concatenate(blocks, axis=0), 0, 0).astype(BF)

        def send_back(d):
            pz = lax.rem(z + d, NZ)
            zro[h, pz] = fold(pz)
            back_copy(h, d).start()

        each(1, NZ, send_back)
        zri[h, z] = fold(z)

    each(0, NH, work)

    def gz_copy(d):
        return remote(gacc, gz.at[z], gzs.at[d], gzr.at[d], device(lax.rem(z + d, NZ), y, c, x))

    def gz_arrival(d):
        pz = lax.rem(z + NZ - d, NZ)
        return remote(gacc, gz.at[pz], gzs.at[d], gzr.at[d], device(pz, y, c, x))

    def gm_copy():
        return remote(gs, gm, gms, gmr, mate)

    def gy_copy(d):
        return remote(gt, gy.at[y], gys.at[d], gyr.at[d], device(z, lax.rem(y + d, NY), c, x))

    def gy_arrival(d):
        py = lax.rem(y + NY - d, NY)
        return remote(gt, gy.at[py], gys.at[d], gyr.at[d], device(z, py, c, x))

    each(1, NZ, lambda d: gz_copy(d).start())
    gz[z] = gacc[...]

    def u_copy(h, i):
        py, px = xy_peer(i)
        return remote(
            uout.at[h, :, py * NX + px], out.at[:, :, columns(y, x, h)], us.at[h, i], ur.at[h, i], device(z, py, c, px)
        )

    def u_arrival(h, i):
        py, px = xy_source(i)
        return remote(
            uout.at[h, :, spot], out.at[:, :, columns(py, px, h)], us.at[h, i], ur.at[h, i], device(z, py, c, px)
        )

    def u_own(h):
        return pltpu.make_async_copy(uout.at[h, :, spot], out.at[:, :, columns(y, x, h)], out_own.at[h])

    def unpool(h):
        each(1, NZ, lambda d: back_arrival(h, d).wait_recv())

        def block(b):
            chosen = place[:, pl.ds(pl.multiple_of(b * 2 * ROWS, 2 * ROWS), 2 * ROWS)]
            found = dot(chosen, zri[h].reshape(NZ * cap, 4 * HD), 0, 0).astype(BF)
            for k in range(2):
                for a in range(4):
                    uout[h, a, b * 2 + k] = found[k * ROWS : (k + 1) * ROWS, a * HD : (a + 1) * HD]

        each(0, POOL // 2, block)
        each(1, POOL, lambda i: u_copy(h, i).start())
        u_own(h).start()

    unpool(0)
    each(1, NZ, lambda d: gz_arrival(d).wait_recv())
    gs[...] = jnp.sum(gz[...], axis=0)
    gm_copy().start()
    unpool(1)
    gm_copy().wait_recv()
    gt[...] = gs[...] + gm[...]
    each(1, NY, lambda d: gy_copy(d).start())
    gy[y] = gt[...]
    unpool(2)
    each(1, NY, lambda d: gy_arrival(d).wait_recv())
    gain_out[...] = gy[...]

    def finish(h):
        def finish_xy(i):
            u_arrival(h, i).wait_recv()
            u_copy(h, i).wait_send()
            xy_copy(h, i).wait_send()

        each(1, POOL, finish_xy)
        u_own(h).wait()

        def finish_z(d):
            z_copy(h, d).wait_send()
            back_copy(h, d).wait_send()

        each(1, NZ, finish_z)
        each(1, NY, lambda d: grad_copy(h, d).wait_send())
        half_copy(h).wait_send()
        res_copy(h).wait_send()

    each(0, NH, finish)
    each(1, NZ, lambda d: gz_copy(d).wait_send())
    gm_copy().wait_send()
    each(1, NY, lambda d: gy_copy(d).wait_send())


def exchange(cap, collective_id, *operands):
    vmem = pltpu.VMEM
    dma = pltpu.SemaphoreType.DMA
    any_spec = pl.BlockSpec(memory_space=pl.ANY)
    vmem_spec = pl.BlockSpec(memory_space=pltpu.VMEM)
    scratch = [
        vmem((3, ROWS, FEATURES), BF),
        vmem((SLOTS, 1536), BF),
        vmem((NH, 4, POOL, ROWS, HD), BF),
        vmem((NH, NY, SLOTS, HD), BF),
        vmem((NH, NZ, cap, 3 * HD), BF),
        vmem((NH, NZ, cap, 3 * HD), BF),
        vmem((NH, NY, HALF, 3 * HD), BF),
        vmem((NH, NY, NC, HALF, 3 * HD), BF),
        vmem((NH, NC, NY, HALF, 4 * HD), BF),
        vmem((NH, NY, HALF, 4 * HD), BF),
        vmem((NH, NZ, cap, 4 * HD), BF),
        vmem((NH, NZ, cap, 4 * HD), BF),
        vmem((NZ * cap, WIDE), BF),
        vmem((NZ, 2 * NY * PART, cap), BF),
        vmem((NY, SLOTS, HD), F32),
        vmem((NY, 8, SLOTS), F32),
        vmem((WIDE, WIDE), BF),
        vmem((SLOTS, SLOTS), BF),
        vmem((NH, 8, HD), F32),
        vmem((NZ, NH, 8, HD), F32),
        vmem((NH, 8, HD), F32),
        vmem((NH, 8, HD), F32),
        vmem((NH, 8, HD), F32),
        vmem((NY, NH, 8, HD), F32),
        dma((4,)),
        dma((NH,)),
        dma((NH,)),
        dma((NH,)),
    ]
    for width in (POOL, POOL, NY, NY, NZ, NZ):
        scratch.append(dma((NH, width)))
    scratch += [dma((NH,)), dma((NH,)), dma((NH,)), dma((NH,))]
    scratch += [dma((NH, NZ)), dma((NH, NZ)), dma((NH, POOL)), dma((NH, POOL))]
    scratch += [dma((NZ,)), dma((NZ,)), dma(()), dma(()), dma((NY,)), dma((NY,))]
    return pl.pallas_call(
        functools.partial(main_kernel, cap),
        name=f"exchange_{cap}",
        out_shape=(
            jax.ShapeDtypeStruct((4, ROWS, FEATURES), BF),
            jax.ShapeDtypeStruct((NY, NH, 8, HD), F32),
        ),
        in_specs=[any_spec] * 4 + [vmem_spec] * 3,
        out_specs=(any_spec, vmem_spec),
        scratch_shapes=scratch,
        compiler_params=pltpu.CompilerParams(
            collective_id=collective_id, has_side_effects=True, vmem_limit_bytes=VMEM_LIMIT
        ),
    )(*operands)


FULL = POOL * NY * NC * 2


def shards(
    query_rows, key_rows, value_rows, destination, image_slot, gain_query, gain_key, grad_output
):
    codes = (destination * 8 + image_slot).reshape(NZ, NY, NC, NX, ROWS)
    codes = codes.transpose(0, 2, 1, 3, 4).reshape(NZ * NC, WIDE)
    operands = (query_rows, key_rows, value_rows, grad_output, gain_query, gain_key, codes)
    out, gains = exchange(FULL, 0, *operands)
    first = lax.axis_index("dp") * 2
    gains = lax.dynamic_slice_in_dim(gains, first, 2, axis=3)
    grad_gain_query = gains[:, :, 0].reshape(NY * NH, 2)
    grad_gain_key = gains[:, :, 1].reshape(NY * NH, 2)
    return (out[0], out[1], out[2], out[3], grad_gain_query, grad_gain_key)


def solution(mesh):
    in_specs = (
        P(("dp", "mp"), None),
        P(("dp", "mp"), None),
        P(("dp", "mp"), None),
        P(),
        P(),
        P("mp", None),
        P("mp", None),
        P("dp", "mp"),
    )
    out_specs = (
        P(("dp", "mp"), None),
        P(("dp", "mp"), None),
        P(("dp", "mp"), None),
        P(("dp", "mp"), None),
        P("mp", "dp"),
        P("mp", "dp"),
    )
    return jax.shard_map(shards, mesh=mesh, in_specs=in_specs, out_specs=out_specs, check_vma=False)
```

```python
import functools
import math

import jax
import jax.numpy as jnp
from jax import lax
from jax.experimental import pallas as pl
from jax.experimental.pallas import tpu as pltpu
from jax.sharding import PartitionSpec as P

NZ, NY, NC, NX = 8, 4, 2, 4
POOL = NY * NX
ROWS = 64
WIDE = POOL * ROWS
HD = 128
NH = 3
SLOTS = 512
HALF = SLOTS // NC
PART = HALF // NZ
FEATURES = 6144
EPSILON = 1e-06
MESH = pl.DeviceIdType.MESH
BF = jnp.bfloat16
F32 = jnp.float32
VMEM_LIMIT = 60 * 1024 * 1024


def iota(shape, dim):
    return lax.broadcasted_iota(jnp.int32, shape, dim)


def dot(a, b, ca=1, cb=0):
    return lax.dot_general(a, b, (((ca,), (cb,)), ((), ())), preferred_element_type=F32)


def onehot(flags):
    return jnp.where(flags, 1.0, 0.0).astype(BF)


def coords():
    dp = lax.axis_index("dp")
    return (lax.div(dp, 8), lax.rem(lax.div(dp, 2), 4), lax.rem(dp, 2), lax.axis_index("mp"))


def device(z, y, c, x):
    return ((z * NY + y) * NC + c, x)


def build_tables(cap, z, c, codes, place, expand, lab_col, lab_row, tri):
    lane = iota((1, WIDE), 1)
    lower, upper = iota((WIDE, WIDE), 0), iota((WIDE, WIDE), 1)
    earlier = lower < upper
    tri[...] = onehot(earlier)
    own = codes[pl.ds(z * NC + c, 1), :]
    own_plane = own >> 6
    planes = own_plane == iota((NZ, WIDE), 0)
    mine = jnp.concatenate([codes[pl.ds(u * NC + c, 1), :] for u in range(NZ)], axis=0)
    members = (mine >> 6) == z
    both = jnp.concatenate([onehot(planes), onehot(members)], axis=0)
    before = dot(both, tri[...])
    own_rank = jnp.sum(jnp.where(planes, before[:NZ], 0.0), axis=0, keepdims=True)
    position = own_rank.astype(jnp.int32) + own_plane * cap
    for step in range(NZ):
        place[pl.ds(step * cap, cap), :] = onehot(position == iota((cap, WIDE), 0) + step * cap)
    message_rank = jnp.where(members, before[NZ:], -1.0).astype(jnp.int32)
    tri[...] = onehot(earlier & ((lower >> 6) == (upper >> 6)))
    order = [(jj, cc) for cc in range(NC) for jj in range(NY)]
    source = (lane >> 6) * 2
    for u in range(NZ):
        for k in range(NC):
            core = c if k == 0 else 1 - c
            row = codes[pl.ds(u * NC + core, 1), :]
            group = iota((NZ, WIDE), 0)
            name = z * 8 + (group & 3) * 2 + jnp.where(group < NY, c, 1 - c)
            member = (row >> 3) == name
            count = dot(onehot(member), tri[...])
            slot = jnp.where(member, count + source.astype(F32), -1.0)
            groups = NZ if k == 0 else NY
            blocks = [slot[g : g + 1, :].astype(jnp.int32) == iota((PART, WIDE), 0) for g in range(groups)]
            chosen = onehot(jnp.concatenate(blocks, axis=0))
            image = jnp.broadcast_to(((row & 7) + 1).astype(F32), (HD, WIDE)).astype(BF)
            label = dot(chosen[: NY * PART], image, 1, 1)
            for g in range(NY):
                at = pl.multiple_of(core * HALF + u * PART, PART)
                found = label[g * PART : (g + 1) * PART]
                empty = -1.0 - (at + iota((PART, HD), 0)).astype(F32)
                lab_col[g, pl.ds(at, PART), :] = jnp.where(found > 0.5, found, empty)
            if k == 0:
                ranks = onehot(message_rank[u : u + 1, :] == iota((cap, WIDE), 0))
                expand[u] = dot(chosen, ranks, 1, 1).astype(BF)
    for g in range(NY):
        lab_row[g] = lab_col[g].T[:8]


def normalize(block):
    floats = block.astype(F32)
    average = jnp.mean(floats, axis=-1, keepdims=True)
    centred = floats - average
    inverse = lax.rsqrt(jnp.mean(centred * centred, axis=-1, keepdims=True) + EPSILON)
    return centred * inverse, inverse


def norm_back(grad_hat, normed, inverse):
    first = jnp.mean(grad_hat, axis=-1, keepdims=True)
    second = jnp.mean(grad_hat * normed, axis=-1, keepdims=True)
    return inverse * (grad_hat - first - normed * second)


def head_pass(query, key, value, cot, gain_q, gain_k, col, row, width=256):
    scale = 1.0 / math.sqrt(HD)
    query_hat, query_inverse = normalize(query)
    key_hat, key_inverse = normalize(key)
    query_low = (query_hat * gain_q).astype(BF)
    key_low = (key_hat * gain_k).astype(BF)
    col = jnp.concatenate([col] * (width // HD), axis=1)
    outs, grads_q = [], []
    grad_v = jnp.zeros((SLOTS, HD), F32)
    grad_k = jnp.zeros((SLOTS, HD), F32)
    for at in range(0, SLOTS, width):
        q = query_low[at : at + width]
        g = cot[at : at + width]
        scores = dot(key_low, q, 1, 1)
        scores = jnp.where(col == row[:, at : at + width], scores, -1e30)
        top = jnp.max(scores, axis=0, keepdims=True)
        weights = jnp.exp((scores - top) * scale)
        attention = weights * (1.0 / jnp.sum(weights, axis=0, keepdims=True))
        low = attention.astype(BF)
        probs = dot(value, g, 1, 1)
        inner = jnp.sum(attention * probs, axis=0, keepdims=True)
        grad_s = (attention * (probs - inner) * scale).astype(BF)
        outs.append(dot(low, value, 0, 0))
        grads_q.append(dot(grad_s, key_low, 0, 0))
        grad_v = grad_v + dot(low, g)
        grad_k = grad_k + dot(grad_s, q)
    grad_q = jnp.concatenate(grads_q, axis=0)
    term_q = jnp.sum(grad_q * query_hat, axis=0, keepdims=True)
    term_k = jnp.sum(grad_k * key_hat, axis=0, keepdims=True)
    back_q = norm_back(grad_q * gain_q, query_hat, query_inverse)
    back_k = norm_back(grad_k * gain_k, key_hat, key_inverse)
    packed = jnp.concatenate(
        [jnp.concatenate(outs, axis=0).astype(BF), back_q.astype(BF), back_k.astype(BF), grad_v.astype(BF)],
        axis=1,
    )
    return packed, term_q, term_k


def main_kernel(
    cap, query_in, key_in, value_in, grad_in, gain_q, gain_k, codes, out, gain_out,
    rows, grads, xin, gob, zout, zin, half_out, packed, res, rin, zro, zri,
    place, expand, lab_col, lab_row, tri, shuffle, gacc, gz, gs, gm, gt, gy,
    load_sem, own_sem, grad_own, out_own, xs, xr, gos, gor, zs, zr, hs, hr, rs, rr, zrs, zrr, us, ur,
    gzs, gzr, gms, gmr, gys, gyr,
):
    uout = xin
    z, y, c, x = coords()
    spot = y * NX + x
    loads = [
        pltpu.make_async_copy(ref, rows.at[k], load_sem.at[k])
        for k, ref in enumerate((query_in, key_in, value_in))
    ]
    loads.append(pltpu.make_async_copy(grad_in, grads, load_sem.at[3]))
    for load in loads:
        load.start()

    barrier = pltpu.get_barrier_semaphore()

    def greet(target):
        pl.semaphore_signal(barrier, inc=1, device_id=target, device_id_type=MESH)

    def xy_peer(i):
        return lax.rem(y + lax.div(i, NX), NY), lax.rem(x + lax.rem(i, NX), NX)

    def xy_source(i):
        return lax.rem(y + NY - lax.div(i, NX), NY), lax.rem(x + NX - lax.rem(i, NX), NX)

    def each(low, high, body):
        def step(i, carry):
            body(i)
            return carry

        lax.fori_loop(low, high, step, 0)

    def greet_xy(i):
        py, px = xy_peer(i)
        greet(device(z, py, c, px))

    def greet_z(d):
        greet(device(lax.rem(z + d, NZ), y, c, x))

    each(1, POOL, greet_xy)
    each(1, NZ, greet_z)
    mate = device(z, y, 1 - c, x)
    greet(mate)
    pl.semaphore_wait(barrier, POOL - 1 + NZ - 1 + 1)

    def remote(src, dst, send, recv, target):
        return pltpu.make_async_remote_copy(
            src_ref=src, dst_ref=dst, send_sem=send, recv_sem=recv, device_id=target, device_id_type=MESH
        )

    def columns(py, px, h):
        return pl.ds(pl.multiple_of(px * 1536 + py * 384 + h * HD, HD), HD)

    def xy_copy(h, i):
        py, px = xy_peer(i)
        return remote(
            rows.at[:, :, columns(py, px, h)], xin.at[h, 0:3, spot], xs.at[h, i], xr.at[h, i], device(z, py, c, px)
        )

    def xy_arrival(h, i):
        py, px = xy_source(i)
        return remote(
            rows.at[:, :, columns(y, x, h)], xin.at[h, 0:3, py * NX + px], xs.at[h, i], xr.at[h, i], device(z, py, c, px)
        )

    def xy_own(h):
        return pltpu.make_async_copy(rows.at[:, :, columns(y, x, h)], xin.at[h, 0:3, spot], own_sem.at[h])

    def grad_columns(py, h):
        return pl.ds(pl.multiple_of(py * 384 + h * HD, HD), HD)

    def grad_copy(h, d):
        py = lax.rem(y + d, NY)
        return remote(grads.at[:, grad_columns(py, h)], gob.at[h, y], gos.at[h, d], gor.at[h, d], device(z, py, c, x))

    def grad_arrival(h, d):
        py = lax.rem(y + NY - d, NY)
        return remote(grads.at[:, grad_columns(y, h)], gob.at[h, py], gos.at[h, d], gor.at[h, d], device(z, py, c, x))

    def grad_keep(h):
        return pltpu.make_async_copy(grads.at[:, grad_columns(y, h)], gob.at[h, y], grad_own.at[h])

    for load in loads:
        load.wait()

    def send_rows(h):
        each(1, POOL, lambda i: xy_copy(h, i).start())
        xy_own(h).start()
        each(1, NY, lambda d: grad_copy(h, d).start())
        grad_keep(h).start()

    each(0, NH, send_rows)

    build_tables(cap, z, c, codes, place, expand, lab_col, lab_row, tri)
    slot = iota((SLOTS, SLOTS), 0)
    pool = (slot >> 1) & 15
    canon = (pool & 3) * 128 + ((slot >> 5) & 7) * 16 + (pool >> 2) * 4 + (slot >> 8) * 2 + (slot & 1)
    shuffle[...] = onehot(canon == iota((SLOTS, SLOTS), 1))
    gacc[...] = jnp.zeros_like(gacc)

    def z_copy(h, d):
        pz = lax.rem(z + d, NZ)
        return remote(zout.at[h, pz], zin.at[h, z], zs.at[h, d], zr.at[h, d], device(pz, y, c, x))

    def z_arrival(h, d):
        pz = lax.rem(z + NZ - d, NZ)
        return remote(zout.at[h, pz], zin.at[h, pz], zs.at[h, d], zr.at[h, d], device(pz, y, c, x))

    def message(h, pz):
        pooled = jnp.concatenate([xin[h, k].reshape(WIDE, HD) for k in range(3)], axis=1)
        chosen = place[pl.ds(pl.multiple_of(pz * cap, 16), cap), :]
        return dot(chosen, pooled).astype(BF)

    def compact(h):
        each(1, POOL, lambda i: xy_arrival(h, i).wait_recv())
        xy_own(h).wait()

        def to_plane(d):
            pz = lax.rem(z + d, NZ)
            zout[h, pz] = message(h, pz)
            z_copy(h, d).start()

        each(1, NZ, to_plane)
        zin[h, z] = message(h, z)

    each(0, NH, compact)

    def half_copy(h):
        return remote(half_out.at[h], packed.at[h, :, c], hs.at[h], hr.at[h], mate)

    def half_arrival(h):
        return remote(half_out.at[h], packed.at[h, :, 1 - c], hs.at[h], hr.at[h], mate)

    def res_copy(h):
        return remote(res.at[h, 1 - c], rin.at[h], rs.at[h], rr.at[h], mate)

    def back_copy(h, d):
        pz = lax.rem(z + d, NZ)
        return remote(zro.at[h, pz], zri.at[h, z], zrs.at[h, d], zrr.at[h, d], device(pz, y, c, x))

    def back_arrival(h, d):
        pz = lax.rem(z + NZ - d, NZ)
        return remote(zro.at[h, pz], zri.at[h, pz], zrs.at[h, d], zrr.at[h, d], device(pz, y, c, x))

    def work(h):
        def unfold(pz):
            spread = dot(expand[pz], zin[h, pz]).astype(BF)
            at = pl.ds(pl.multiple_of(pz * PART, PART), PART)
            for g in range(NY):
                packed[h, g, c, at, :] = spread[g * PART : (g + 1) * PART]
                half_out[h, g, at, :] = spread[(NY + g) * PART : (NY + g + 1) * PART]

        unfold(z)

        def arrive(d):
            z_arrival(h, d).wait_recv()
            unfold(lax.rem(z + NZ - d, NZ))

        each(1, NZ, arrive)
        half_copy(h).start()
        each(1, NY, lambda d: grad_arrival(h, d).wait_recv())
        grad_keep(h).wait()
        half_arrival(h).wait_recv()

        head = y * NH + h
        own_gain_q = gain_q[pl.ds(head, 1), :]
        own_gain_k = gain_k[pl.ds(head, 1), :]

        def group(g):
            block = packed[h, g].reshape(SLOTS, 3 * HD)
            col = lab_col[g]
            cot = dot(shuffle[...], gob[h, g])
            cot = jnp.where(col > 0.0, cot, 0.0).astype(BF)
            result, term_q, term_k = head_pass(
                block[:, :HD], block[:, HD : 2 * HD], block[:, 2 * HD :], cot,
                own_gain_q, own_gain_k, col, lab_row[g, 0:1, :],
            )
            res[h, 0, g] = result[:HALF]
            res[h, 1, g] = result[HALF:]
            gacc[h, 0:1, :] += term_q
            gacc[h, 1:2, :] += term_k

        each(0, NY, group)
        res_copy(h).start()
        res_copy(h).wait_recv()

        def fold(pz):
            at = pl.ds(pl.multiple_of(pz * PART, PART), PART)
            blocks = [res[h, c, g, at, :] for g in range(NY)] + [rin[h, g, at, :] for g in range(NY)]
            return dot(expand[pz], jnp.concatenate(blocks, axis=0), 0, 0).astype(BF)

        def send_back(d):
            pz = lax.rem(z + d, NZ)
            zro[h, pz] = fold(pz)
            back_copy(h, d).start()

        each(1, NZ, send_back)
        zri[h, z] = fold(z)

    each(0, NH, work)

    def gz_copy(d):
        return remote(gacc, gz.at[z], gzs.at[d], gzr.at[d], device(lax.rem(z + d, NZ), y, c, x))

    def gz_arrival(d):
        pz = lax.rem(z + NZ - d, NZ)
        return remote(gacc, gz.at[pz], gzs.at[d], gzr.at[d], device(pz, y, c, x))

    def gm_copy():
        return remote(gs, gm, gms, gmr, mate)

    def gy_copy(d):
        return remote(gt, gy.at[y], gys.at[d], gyr.at[d], device(z, lax.rem(y + d, NY), c, x))

    def gy_arrival(d):
        py = lax.rem(y + NY - d, NY)
        return remote(gt, gy.at[py], gys.at[d], gyr.at[d], device(z, py, c, x))

    each(1, NZ, lambda d: gz_copy(d).start())
    gz[z] = gacc[...]

    def u_copy(h, i):
        py, px = xy_peer(i)
        return remote(
            uout.at[h, :, py * NX + px], out.at[:, :, columns(y, x, h)], us.at[h, i], ur.at[h, i], device(z, py, c, px)
        )

    def u_arrival(h, i):
        py, px = xy_source(i)
        return remote(
            uout.at[h, :, spot], out.at[:, :, columns(py, px, h)], us.at[h, i], ur.at[h, i], device(z, py, c, px)
        )

    def u_own(h):
        return pltpu.make_async_copy(uout.at[h, :, spot], out.at[:, :, columns(y, x, h)], out_own.at[h])

    def unpool(h):
        each(1, NZ, lambda d: back_arrival(h, d).wait_recv())

        def block(b):
            chosen = place[:, pl.ds(pl.multiple_of(b * 2 * ROWS, 2 * ROWS), 2 * ROWS)]
            found = dot(chosen, zri[h].reshape(NZ * cap, 4 * HD), 0, 0).astype(BF)
            for k in range(2):
                for a in range(4):
                    uout[h, a, b * 2 + k] = found[k * ROWS : (k + 1) * ROWS, a * HD : (a + 1) * HD]

        each(0, POOL // 2, block)
        each(1, POOL, lambda i: u_copy(h, i).start())
        u_own(h).start()

    unpool(0)
    each(1, NZ, lambda d: gz_arrival(d).wait_recv())
    gs[...] = jnp.sum(gz[...], axis=0)
    gm_copy().start()
    unpool(1)
    gm_copy().wait_recv()
    gt[...] = gs[...] + gm[...]
    each(1, NY, lambda d: gy_copy(d).start())
    gy[y] = gt[...]
    unpool(2)
    each(1, NY, lambda d: gy_arrival(d).wait_recv())
    gain_out[...] = gy[...]

    def finish(h):
        def finish_xy(i):
            u_arrival(h, i).wait_recv()
            u_copy(h, i).wait_send()
            xy_copy(h, i).wait_send()

        each(1, POOL, finish_xy)
        u_own(h).wait()

        def finish_z(d):
            z_copy(h, d).wait_send()
            back_copy(h, d).wait_send()

        each(1, NZ, finish_z)
        each(1, NY, lambda d: grad_copy(h, d).wait_send())
        half_copy(h).wait_send()
        res_copy(h).wait_send()

    each(0, NH, finish)
    each(1, NZ, lambda d: gz_copy(d).wait_send())
    gm_copy().wait_send()
    each(1, NY, lambda d: gy_copy(d).wait_send())


def exchange(cap, collective_id, *operands):
    vmem = pltpu.VMEM
    dma = pltpu.SemaphoreType.DMA
    any_spec = pl.BlockSpec(memory_space=pl.ANY)
    vmem_spec = pl.BlockSpec(memory_space=pltpu.VMEM)
    scratch = [
        vmem((3, ROWS, FEATURES), BF),
        vmem((SLOTS, 1536), BF),
        vmem((NH, 4, POOL, ROWS, HD), BF),
        vmem((NH, NY, SLOTS, HD), BF),
        vmem((NH, NZ, cap, 3 * HD), BF),
        vmem((NH, NZ, cap, 3 * HD), BF),
        vmem((NH, NY, HALF, 3 * HD), BF),
        vmem((NH, NY, NC, HALF, 3 * HD), BF),
        vmem((NH, NC, NY, HALF, 4 * HD), BF),
        vmem((NH, NY, HALF, 4 * HD), BF),
        vmem((NH, NZ, cap, 4 * HD), BF),
        vmem((NH, NZ, cap, 4 * HD), BF),
        vmem((NZ * cap, WIDE), BF),
        vmem((NZ, 2 * NY * PART, cap), BF),
        vmem((NY, SLOTS, HD), F32),
        vmem((NY, 8, SLOTS), F32),
        vmem((WIDE, WIDE), BF),
        vmem((SLOTS, SLOTS), BF),
        vmem((NH, 8, HD), F32),
        vmem((NZ, NH, 8, HD), F32),
        vmem((NH, 8, HD), F32),
        vmem((NH, 8, HD), F32),
        vmem((NH, 8, HD), F32),
        vmem((NY, NH, 8, HD), F32),
        dma((4,)),
        dma((NH,)),
        dma((NH,)),
        dma((NH,)),
    ]
    for width in (POOL, POOL, NY, NY, NZ, NZ):
        scratch.append(dma((NH, width)))
    scratch += [dma((NH,)), dma((NH,)), dma((NH,)), dma((NH,))]
    scratch += [dma((NH, NZ)), dma((NH, NZ)), dma((NH, POOL)), dma((NH, POOL))]
    scratch += [dma((NZ,)), dma((NZ,)), dma(()), dma(()), dma((NY,)), dma((NY,))]
    return pl.pallas_call(
        functools.partial(main_kernel, cap),
        name=f"exchange_{cap}",
        out_shape=(
            jax.ShapeDtypeStruct((4, ROWS, FEATURES), BF),
            jax.ShapeDtypeStruct((NY, NH, 8, HD), F32),
        ),
        in_specs=[any_spec] * 4 + [vmem_spec] * 3,
        out_specs=(any_spec, vmem_spec),
        scratch_shapes=scratch,
        compiler_params=pltpu.CompilerParams(
            collective_id=collective_id, has_side_effects=True, vmem_limit_bytes=VMEM_LIMIT
        ),
    )(*operands)


ROOMS = (160, 176, POOL * NY * NC * 2)


def shards(
    query_rows, key_rows, value_rows, destination, image_slot, gain_query, gain_key, grad_output
):
    codes = (destination * 8 + image_slot).reshape(NZ, NY, NC, NX, ROWS)
    codes = codes.transpose(0, 2, 1, 3, 4).reshape(NZ * NC, WIDE)
    operands = (query_rows, key_rows, value_rows, grad_output, gain_query, gain_key, codes)
    planes = codes[:, None, :] >> 6 == jnp.arange(NZ, dtype=jnp.int32)[None, :, None]
    most = jnp.max(jnp.sum(planes.astype(jnp.int32), axis=-1))
    level = sum((most > room).astype(jnp.int32) for room in ROOMS[:-1])
    branches = [functools.partial(exchange, room, k) for k, room in enumerate(ROOMS)]
    out, gains = lax.switch(level, branches, *operands)
    first = lax.axis_index("dp") * 2
    gains = lax.dynamic_slice_in_dim(gains, first, 2, axis=3)
    grad_gain_query = gains[:, :, 0].reshape(NY * NH, 2)
    grad_gain_key = gains[:, :, 1].reshape(NY * NH, 2)
    return (out[0], out[1], out[2], out[3], grad_gain_query, grad_gain_key)


def solution(mesh):
    in_specs = (
        P(("dp", "mp"), None),
        P(("dp", "mp"), None),
        P(("dp", "mp"), None),
        P(),
        P(),
        P("mp", None),
        P("mp", None),
        P("dp", "mp"),
    )
    out_specs = (
        P(("dp", "mp"), None),
        P(("dp", "mp"), None),
        P(("dp", "mp"), None),
        P(("dp", "mp"), None),
        P("mp", "dp"),
        P("mp", "dp"),
    )
    return jax.shard_map(shards, mesh=mesh, in_specs=in_specs, out_specs=out_specs, check_vma=False)
```

```python
import functools
import math

import jax
import jax.numpy as jnp
from jax import lax
from jax.experimental import pallas as pl
from jax.experimental.pallas import tpu as pltpu
from jax.sharding import PartitionSpec as P

NZ, NY, NC, NX = 8, 4, 2, 4
POOL = NY * NX
ROWS = 64
WIDE = POOL * ROWS
HD = 128
NH = 3
SLOTS = 512
HALF = SLOTS // NC
PART = HALF // NZ
FEATURES = 6144
EPSILON = 1e-06
MESH = pl.DeviceIdType.MESH
BF = jnp.bfloat16
F32 = jnp.float32
OUTWARD = ((0, 0, 1), (0, 1, 1), (0, 2, 1), (1, 0, 3), (2, 0, 3))
BACKWARD = ((0, 0, 2), (0, 2, 2), (1, 0, 2), (1, 2, 2), (2, 0, 2), (2, 2, 2))
AFTER = (None, None, None, 0, 1, 2)
VMEM_LIMIT = 60 * 1024 * 1024


def iota(shape, dim):
    return lax.broadcasted_iota(jnp.int32, shape, dim)


def dot(a, b, ca=1, cb=0):
    return lax.dot_general(a, b, (((ca,), (cb,)), ((), ())), preferred_element_type=F32)


def onehot(flags):
    return jnp.where(flags, 1.0, 0.0).astype(BF)


def coords():
    dp = lax.axis_index("dp")
    return (lax.div(dp, 8), lax.rem(lax.div(dp, 2), 4), lax.rem(dp, 2), lax.axis_index("mp"))


def device(z, y, c, x):
    return ((z * NY + y) * NC + c, x)


def build_place(cap, z, c, codes, place, tri):
    lower, upper = iota((WIDE, WIDE), 0), iota((WIDE, WIDE), 1)
    earlier = lower < upper
    tri[...] = onehot(earlier)
    own = codes[pl.ds(z * NC + c, 1), :]
    own_plane = own >> 6
    planes = own_plane == iota((NZ, WIDE), 0)
    mine = jnp.concatenate([codes[pl.ds(u * NC + c, 1), :] for u in range(NZ)], axis=0)
    members = (mine >> 6) == z
    both = jnp.concatenate([onehot(planes), onehot(members)], axis=0)
    before = dot(both, tri[...])
    own_rank = jnp.sum(jnp.where(planes, before[:NZ], 0.0), axis=0, keepdims=True)
    position = own_rank.astype(jnp.int32) + own_plane * cap
    for step in range(NZ):
        place[pl.ds(step * cap, cap), :] = onehot(position == iota((cap, WIDE), 0) + step * cap)
    return position, jnp.where(members, before[NZ:], -1.0).astype(jnp.int32)


def build_expand(cap, z, c, position, message_rank, codes, turned, expand, lab_col, lab_row, tri):
    column = jnp.broadcast_to(position.astype(F32), (HD, WIDE)).T
    for k in range(0, NZ * cap, HD):
        turned[:, k : k + HD] = onehot(column == (iota((WIDE, HD), 1) + k).astype(F32))
    lane = iota((1, WIDE), 1)
    lower, upper = iota((WIDE, WIDE), 0), iota((WIDE, WIDE), 1)
    earlier = lower < upper
    tri[...] = onehot(earlier & ((lower >> 6) == (upper >> 6)))
    source = (lane >> 6) * 2
    for u in range(NZ):
        for k in range(NC):
            core = c if k == 0 else 1 - c
            row = codes[pl.ds(u * NC + core, 1), :]
            group = iota((NZ, WIDE), 0)
            name = z * 8 + (group & 3) * 2 + jnp.where(group < NY, c, 1 - c)
            member = (row >> 3) == name
            count = dot(onehot(member), tri[...])
            slot = jnp.where(member, count + source.astype(F32), -1.0)
            groups = NZ if k == 0 else NY
            blocks = [slot[g : g + 1, :].astype(jnp.int32) == iota((PART, WIDE), 0) for g in range(groups)]
            chosen = onehot(jnp.concatenate(blocks, axis=0))
            image = jnp.broadcast_to(((row & 7) + 1).astype(F32), (HD, WIDE)).astype(BF)
            label = dot(chosen[: NY * PART], image, 1, 1)
            for g in range(NY):
                at = pl.multiple_of(core * HALF + u * PART, PART)
                found = label[g * PART : (g + 1) * PART]
                empty = -1.0 - (at + iota((PART, HD), 0)).astype(F32)
                lab_col[g, pl.ds(at, PART), :] = jnp.where(found > 0.5, found, empty)
            if k == 0:
                ranks = onehot(message_rank[u : u + 1, :] == iota((cap, WIDE), 0))
                expand[u] = dot(chosen, ranks, 1, 1).astype(BF)
    for g in range(NY):
        lab_row[g] = lab_col[g].T[:8]


def normalize(block):
    floats = block.astype(F32)
    average = jnp.mean(floats, axis=-1, keepdims=True)
    centred = floats - average
    inverse = lax.rsqrt(jnp.mean(centred * centred, axis=-1, keepdims=True) + EPSILON)
    return centred * inverse, inverse


def norm_back(grad_hat, normed, inverse):
    first = jnp.mean(grad_hat, axis=-1, keepdims=True)
    second = jnp.mean(grad_hat * normed, axis=-1, keepdims=True)
    return inverse * (grad_hat - first - normed * second)


def head_pass(query, key, value, cot, gain_q, gain_k, col, row, width=256):
    scale = 1.0 / math.sqrt(HD)
    query_hat, query_inverse = normalize(query)
    key_hat, key_inverse = normalize(key)
    query_low = (query_hat * gain_q).astype(BF)
    key_low = (key_hat * gain_k).astype(BF)
    col = jnp.concatenate([col] * (width // HD), axis=1)
    outs, grads_q = [], []
    grad_v = jnp.zeros((SLOTS, HD), F32)
    grad_k = jnp.zeros((SLOTS, HD), F32)
    for at in range(0, SLOTS, width):
        q = query_low[at : at + width]
        g = cot[at : at + width]
        scores = dot(key_low, q, 1, 1)
        scores = jnp.where(col == row[:, at : at + width], scores, -1e30)
        top = jnp.max(scores, axis=0, keepdims=True)
        weights = jnp.exp((scores - top) * scale)
        attention = weights * (1.0 / jnp.sum(weights, axis=0, keepdims=True))
        low = attention.astype(BF)
        probs = dot(value, g, 1, 1)
        inner = jnp.sum(attention * probs, axis=0, keepdims=True)
        grad_s = (attention * (probs - inner) * scale).astype(BF)
        outs.append(dot(low, value, 0, 0))
        grads_q.append(dot(grad_s, key_low, 0, 0))
        grad_v = grad_v + dot(low, g)
        grad_k = grad_k + dot(grad_s, q)
    grad_q = jnp.concatenate(grads_q, axis=0)
    term_q = jnp.sum(grad_q * query_hat, axis=0, keepdims=True)
    term_k = jnp.sum(grad_k * key_hat, axis=0, keepdims=True)
    back_q = norm_back(grad_q * gain_q, query_hat, query_inverse)
    back_k = norm_back(grad_k * gain_k, key_hat, key_inverse)
    packed = jnp.concatenate(
        [jnp.concatenate(outs, axis=0).astype(BF), back_q.astype(BF), back_k.astype(BF), grad_v.astype(BF)],
        axis=1,
    )
    return packed, term_q, term_k


def main_kernel(
    cap, query_in, key_in, value_in, grad_in, gain_q, gain_k, codes, out, gain_out,
    rows, grads, xin, gob, zin, half_out, packed, res, rin, zro, zri,
    place, turned, expand, lab_col, lab_row, tri, shuffle, gacc, gz, gs, gm, gt, gy,
    load_sem, own_sem, grad_own, out_own, xs, xr, gos, gor, zs, zr, hs, hr, rs, rr, zrs, zrr, us, ur,
    gzs, gzr, gms, gmr, gys, gyr,
):
    uout = xin
    zout = zro
    z, y, c, x = coords()
    spot = y * NX + x
    loads = [
        pltpu.make_async_copy(ref, rows.at[k], load_sem.at[k])
        for k, ref in enumerate((query_in, key_in, value_in))
    ]
    loads.append(pltpu.make_async_copy(grad_in, grads, load_sem.at[3]))
    for load in loads:
        load.start()

    barrier = pltpu.get_barrier_semaphore()

    def greet(target):
        pl.semaphore_signal(barrier, inc=1, device_id=target, device_id_type=MESH)

    def xy_peer(i):
        return lax.rem(y + lax.div(i, NX), NY), lax.rem(x + lax.rem(i, NX), NX)

    def xy_source(i):
        return lax.rem(y + NY - lax.div(i, NX), NY), lax.rem(x + NX - lax.rem(i, NX), NX)

    def each(low, high, body):
        def step(i, carry):
            body(i)
            return carry

        lax.fori_loop(low, high, step, 0)

    def greet_xy(i):
        py, px = xy_peer(i)
        greet(device(z, py, c, px))

    def greet_z(d):
        greet(device(lax.rem(z + d, NZ), y, c, x))

    each(1, POOL, greet_xy)
    each(1, NZ, greet_z)
    mate = device(z, y, 1 - c, x)
    greet(mate)
    pl.semaphore_wait(barrier, POOL - 1 + NZ - 1 + 1)

    def remote(src, dst, send, recv, target):
        return pltpu.make_async_remote_copy(
            src_ref=src, dst_ref=dst, send_sem=send, recv_sem=recv, device_id=target, device_id_type=MESH
        )

    def columns(py, px, h):
        return pl.ds(pl.multiple_of(px * 1536 + py * 384 + h * HD, HD), HD)

    def lanes(a, n):
        return pl.ds(a * HD, n * HD)

    def xy_copy(f, i):
        h, a, n = OUTWARD[f]
        py, px = xy_peer(i)
        return remote(
            rows.at[a : a + n, :, columns(py, px, h)], xin.at[h, a : a + n, spot],
            xs.at[f, i], xr.at[f, i], device(z, py, c, px),
        )

    def xy_arrival(f, i):
        h, a, n = OUTWARD[f]
        py, px = xy_source(i)
        return remote(
            rows.at[a : a + n, :, columns(y, x, h)], xin.at[h, a : a + n, py * NX + px],
            xs.at[f, i], xr.at[f, i], device(z, py, c, px),
        )

    def xy_own(f):
        h, a, n = OUTWARD[f]
        return pltpu.make_async_copy(
            rows.at[a : a + n, :, columns(y, x, h)], xin.at[h, a : a + n, spot], own_sem.at[f]
        )

    def grad_columns(py, h):
        return pl.ds(pl.multiple_of(py * 384 + h * HD, HD), HD)

    def grad_copy(h, d):
        py = lax.rem(y + d, NY)
        return remote(grads.at[:, grad_columns(py, h)], gob.at[h, y], gos.at[h, d], gor.at[h, d], device(z, py, c, x))

    def grad_arrival(h, d):
        py = lax.rem(y + NY - d, NY)
        return remote(grads.at[:, grad_columns(y, h)], gob.at[h, py], gos.at[h, d], gor.at[h, d], device(z, py, c, x))

    def grad_keep(h):
        return pltpu.make_async_copy(grads.at[:, grad_columns(y, h)], gob.at[h, y], grad_own.at[h])

    def send_rows(f):
        each(1, POOL, lambda i: xy_copy(f, i).start())
        xy_own(f).start()

    def send_grads(h):
        each(1, NY, lambda d: grad_copy(h, d).start())
        grad_keep(h).start()

    for k in range(3):
        loads[k].wait()
        send_rows(k)
    loads[3].wait()
    position, message_rank = build_place(cap, z, c, codes, place, tri)
    slot = iota((SLOTS, SLOTS), 0)
    pool = (slot >> 1) & 15
    canon = (pool & 3) * 128 + ((slot >> 5) & 7) * 16 + (pool >> 2) * 4 + (slot >> 8) * 2 + (slot & 1)
    shuffle[...] = onehot(canon == iota((SLOTS, SLOTS), 1))
    gacc[...] = jnp.zeros_like(gacc)

    def z_copy(f, d):
        h, a, n = OUTWARD[f]
        pz = lax.rem(z + d, NZ)
        return remote(
            zout.at[h, pz, :, lanes(a, n)], zin.at[h, z, :, lanes(a, n)], zs.at[f, d], zr.at[f, d], device(pz, y, c, x)
        )

    def z_arrival(f, d):
        h, a, n = OUTWARD[f]
        pz = lax.rem(z + NZ - d, NZ)
        return remote(
            zout.at[h, pz, :, lanes(a, n)], zin.at[h, pz, :, lanes(a, n)], zs.at[f, d], zr.at[f, d], device(pz, y, c, x)
        )

    def message(f, pz):
        h, a, n = OUTWARD[f]
        pooled = jnp.concatenate([xin[h, k].reshape(WIDE, HD) for k in range(a, a + n)], axis=1)
        chosen = place[pl.ds(pl.multiple_of(pz * cap, 16), cap), :]
        return dot(chosen, pooled).astype(BF)

    def receive_rows(f):
        each(1, POOL, lambda i: xy_arrival(f, i).wait_recv())
        xy_own(f).wait()

    def compact(f):
        h, a, n = OUTWARD[f]
        part = slice(a * HD, (a + n) * HD)

        def to_plane(d):
            pz = lax.rem(z + d, NZ)
            zout[h, pz, :, part] = message(f, pz)
            z_copy(f, d).start()

        each(1, NZ, to_plane)
        zin[h, z, :, part] = message(f, z)

    receive_rows(0)
    compact(0)
    receive_rows(1)
    send_rows(3)
    compact(1)
    receive_rows(2)
    send_grads(0)
    compact(2)
    build_expand(cap, z, c, position, message_rank, codes, turned, expand, lab_col, lab_row, tri)
    receive_rows(3)
    send_rows(4)
    send_grads(1)
    compact(3)
    receive_rows(4)
    send_grads(2)
    compact(4)

    def half_copy(h):
        return remote(half_out, packed.at[h, :, c], hs.at[h], hr.at[h], mate)

    def half_arrival(h):
        return remote(half_out, packed.at[h, :, 1 - c], hs.at[h], hr.at[h], mate)

    def res_copy(h):
        return remote(res.at[1 - c], rin, rs.at[h], rr.at[h], mate)

    def back_copy(b, d):
        h, a, n = BACKWARD[b]
        pz = lax.rem(z + d, NZ)
        return remote(
            zro.at[h, pz, :, lanes(a, n)], zri.at[h, z, :, lanes(a, n)], zrs.at[b, d], zrr.at[b, d], device(pz, y, c, x)
        )

    def back_arrival(b, d):
        h, a, n = BACKWARD[b]
        pz = lax.rem(z + NZ - d, NZ)
        return remote(
            zro.at[h, pz, :, lanes(a, n)], zri.at[h, pz, :, lanes(a, n)], zrs.at[b, d], zrr.at[b, d], device(pz, y, c, x)
        )

    def work(h):
        def unfold(pz):
            spread = dot(expand[pz], zin[h, pz]).astype(BF)
            at = pl.ds(pl.multiple_of(pz * PART, PART), PART)
            for g in range(NY):
                packed[h, g, c, at, :] = spread[g * PART : (g + 1) * PART]
                half_out[g, at, :] = spread[(NY + g) * PART : (NY + g + 1) * PART]

        unfold(z)

        def arrive(d):
            for f, piece in enumerate(OUTWARD):
                if piece[0] == h:
                    z_arrival(f, d).wait_recv()
            unfold(lax.rem(z + NZ - d, NZ))

        each(1, NZ, arrive)
        half_copy(h).start()
        each(1, NY, lambda d: grad_arrival(h, d).wait_recv())
        grad_keep(h).wait()
        half_arrival(h).wait_recv()

        head = y * NH + h
        own_gain_q = gain_q[pl.ds(head, 1), :]
        own_gain_k = gain_k[pl.ds(head, 1), :]

        def group(g):
            block = packed[h, g].reshape(SLOTS, 3 * HD)
            col = lab_col[g]
            cot = dot(shuffle[...], gob[h, g])
            cot = jnp.where(col > 0.0, cot, 0.0).astype(BF)
            result, term_q, term_k = head_pass(
                block[:, :HD], block[:, HD : 2 * HD], block[:, 2 * HD :], cot,
                own_gain_q, own_gain_k, col, lab_row[g, 0:1, :],
            )
            res[0, g] = result[:HALF]
            res[1, g] = result[HALF:]
            gacc[h, 0:1, :] += term_q
            gacc[h, 1:2, :] += term_k

        each(0, NY, group)
        res_copy(h).start()
        res_copy(h).wait()
        half_copy(h).wait_send()

    def send_back(b):
        h, a, n = BACKWARD[b]
        part = slice(a * HD, (a + n) * HD)

        def fold(pz):
            at = pl.ds(pl.multiple_of(pz * PART, PART), PART)
            blocks = [res[c, g, at, part] for g in range(NY)] + [rin[g, at, part] for g in range(NY)]
            return dot(expand[pz], jnp.concatenate(blocks, axis=0), 0, 0).astype(BF)

        def to_plane(d):
            pz = lax.rem(z + d, NZ)
            zro[h, pz, :, part] = fold(pz)
            back_copy(b, d).start()

        each(1, NZ, to_plane)
        zri[h, z, :, part] = fold(z)

    def gz_copy(d):
        return remote(gacc, gz.at[z], gzs.at[d], gzr.at[d], device(lax.rem(z + d, NZ), y, c, x))

    def gz_arrival(d):
        pz = lax.rem(z + NZ - d, NZ)
        return remote(gacc, gz.at[pz], gzs.at[d], gzr.at[d], device(pz, y, c, x))

    def gm_copy():
        return remote(gs, gm, gms, gmr, mate)

    def gy_copy(d):
        return remote(gt, gy.at[y], gys.at[d], gyr.at[d], device(z, lax.rem(y + d, NY), c, x))

    def gy_arrival(d):
        py = lax.rem(y + NY - d, NY)
        return remote(gt, gy.at[py], gys.at[d], gyr.at[d], device(z, py, c, x))

    def u_copy(b, i):
        h, a, n = BACKWARD[b]
        py, px = xy_peer(i)
        return remote(
            uout.at[h, a : a + n, py * NX + px], out.at[a : a + n, :, columns(y, x, h)],
            us.at[b, i], ur.at[b, i], device(z, py, c, px),
        )

    def u_arrival(b, i):
        h, a, n = BACKWARD[b]
        py, px = xy_source(i)
        return remote(
            uout.at[h, a : a + n, spot], out.at[a : a + n, :, columns(py, px, h)],
            us.at[b, i], ur.at[b, i], device(z, py, c, px),
        )

    def u_own(b):
        h, a, n = BACKWARD[b]
        return pltpu.make_async_copy(
            uout.at[h, a : a + n, spot], out.at[a : a + n, :, columns(y, x, h)], out_own.at[b]
        )

    def unpool(b):
        h, a, n = BACKWARD[b]
        each(1, NZ, lambda d: back_arrival(b, d).wait_recv())

        def block(k):
            chosen = turned[pl.ds(pl.multiple_of(k * 4 * ROWS, 4 * ROWS), 4 * ROWS), :]
            replies = zri[h, :, :, a * HD : (a + n) * HD].reshape(NZ * cap, n * HD)
            found = dot(chosen, replies).astype(BF)
            for r in range(4):
                for m in range(n):
                    uout[h, a + m, k * 4 + r] = found[r * ROWS : (r + 1) * ROWS, m * HD : (m + 1) * HD]

        each(0, POOL // 4, block)
        each(1, POOL, lambda i: u_copy(b, i).start())
        u_own(b).start()

    left = set()

    def leave(b):
        if b is not None and b not in left:
            left.add(b)
            each(1, NZ, lambda d: back_copy(b, d).wait_send())

    def finish_messages(h):
        for f, piece in enumerate(OUTWARD):
            if piece[0] == h:
                each(1, NZ, lambda d, f=f: z_copy(f, d).wait_send())

    def finish(h):
        each(1, NY, lambda d: grad_copy(h, d).wait_send())

    def finish_back(b):
        def finish_xy(i):
            u_arrival(b, i).wait_recv()
            u_copy(b, i).wait_send()

        leave(b)
        each(1, POOL, finish_xy)
        u_own(b).wait()

    count = len(BACKWARD)
    ready = 0
    given = 0
    for h in range(NH):
        work(h)
        finish_messages(h)
        if h == NH - 1:
            each(1, NZ, lambda d: gz_copy(d).start())
            gz[z] = gacc[...]
        while ready < count and BACKWARD[ready][0] == h:
            after = AFTER[ready]
            if after is not None:
                leave(after)
            send_back(ready)
            ready += 1
            if after is not None:
                while given <= after:
                    unpool(given)
                    given += 1

    each(1, NZ, lambda d: gz_arrival(d).wait_recv())
    gs[...] = jnp.sum(gz[...], axis=0)
    gm_copy().start()
    for f in range(len(OUTWARD)):
        each(1, POOL, lambda i, f=f: xy_copy(f, i).wait_send())
    each(0, NH, finish)
    gm_copy().wait_recv()
    gt[...] = gs[...] + gm[...]
    each(1, NY, lambda d: gy_copy(d).start())
    gy[y] = gt[...]
    while given < count - 1:
        unpool(given)
        given += 1
    each(1, NY, lambda d: gy_arrival(d).wait_recv())
    gain_out[...] = gy[...]
    each(1, NZ, lambda d: gz_copy(d).wait_send())
    gm_copy().wait_send()
    each(1, NY, lambda d: gy_copy(d).wait_send())
    for b in range(count - 3):
        finish_back(b)
    unpool(count - 1)
    for b in range(count - 3, count):
        finish_back(b)


def exchange(cap, collective_id, *operands):
    outward, backward = len(OUTWARD), len(BACKWARD)
    vmem = pltpu.VMEM
    dma = pltpu.SemaphoreType.DMA
    any_spec = pl.BlockSpec(memory_space=pl.ANY)
    vmem_spec = pl.BlockSpec(memory_space=pltpu.VMEM)
    scratch = [
        vmem((3, ROWS, FEATURES), BF),
        vmem((SLOTS, 1536), BF),
        vmem((NH, 4, POOL, ROWS, HD), BF),
        vmem((NH, NY, SLOTS, HD), BF),
        vmem((NH, NZ, cap, 3 * HD), BF),
        vmem((NY, HALF, 3 * HD), BF),
        vmem((NH, NY, NC, HALF, 3 * HD), BF),
        vmem((NC, NY, HALF, 4 * HD), BF),
        vmem((NY, HALF, 4 * HD), BF),
        vmem((NH, NZ, cap, 4 * HD), BF),
        vmem((NH, NZ, cap, 4 * HD), BF),
        vmem((NZ * cap, WIDE), BF),
        vmem((WIDE, NZ * cap), BF),
        vmem((NZ, 2 * NY * PART, cap), BF),
        vmem((NY, SLOTS, HD), F32),
        vmem((NY, 8, SLOTS), F32),
        vmem((WIDE, WIDE), BF),
        vmem((SLOTS, SLOTS), BF),
        vmem((NH, 8, HD), F32),
        vmem((NZ, NH, 8, HD), F32),
        vmem((NH, 8, HD), F32),
        vmem((NH, 8, HD), F32),
        vmem((NH, 8, HD), F32),
        vmem((NY, NH, 8, HD), F32),
        dma((4,)),
        dma((outward,)),
        dma((NH,)),
        dma((backward,)),
        dma((outward, POOL)),
        dma((outward, POOL)),
        dma((NH, NY)),
        dma((NH, NY)),
        dma((outward, NZ)),
        dma((outward, NZ)),
    ]
    scratch += [dma((NH,)), dma((NH,)), dma((NH,)), dma((NH,))]
    scratch += [dma((backward, NZ)), dma((backward, NZ)), dma((backward, POOL)), dma((backward, POOL))]
    scratch += [dma((NZ,)), dma((NZ,)), dma(()), dma(()), dma((NY,)), dma((NY,))]
    return pl.pallas_call(
        functools.partial(main_kernel, cap),
        name=f"exchange_{cap}",
        out_shape=(
            jax.ShapeDtypeStruct((4, ROWS, FEATURES), BF),
            jax.ShapeDtypeStruct((NY, NH, 8, HD), F32),
        ),
        in_specs=[any_spec] * 4 + [vmem_spec] * 3,
        out_specs=(any_spec, vmem_spec),
        scratch_shapes=scratch,
        compiler_params=pltpu.CompilerParams(
            collective_id=collective_id, has_side_effects=True, vmem_limit_bytes=VMEM_LIMIT
        ),
    )(*operands)


ROOMS = (160, 176, POOL * NY * NC * 2)


def shards(
    query_rows, key_rows, value_rows, destination, image_slot, gain_query, gain_key, grad_output
):
    codes = (destination * 8 + image_slot).reshape(NZ, NY, NC, NX, ROWS)
    codes = codes.transpose(0, 2, 1, 3, 4).reshape(NZ * NC, WIDE)
    operands = (query_rows, key_rows, value_rows, grad_output, gain_query, gain_key, codes)
    planes = codes[:, None, :] >> 6 == jnp.arange(NZ, dtype=jnp.int32)[None, :, None]
    most = jnp.max(jnp.sum(planes.astype(jnp.int32), axis=-1))
    level = sum((most > room).astype(jnp.int32) for room in ROOMS[:-1])
    branches = [functools.partial(exchange, room, k) for k, room in enumerate(ROOMS)]
    out, gains = lax.switch(level, branches, *operands)
    first = lax.axis_index("dp") * 2
    gains = lax.dynamic_slice_in_dim(gains, first, 2, axis=3)
    grad_gain_query = gains[:, :, 0].reshape(NY * NH, 2)
    grad_gain_key = gains[:, :, 1].reshape(NY * NH, 2)
    return (out[0], out[1], out[2], out[3], grad_gain_query, grad_gain_key)


def solution(mesh):
    in_specs = (
        P(("dp", "mp"), None),
        P(("dp", "mp"), None),
        P(("dp", "mp"), None),
        P(),
        P(),
        P("mp", None),
        P("mp", None),
        P("dp", "mp"),
    )
    out_specs = (
        P(("dp", "mp"), None),
        P(("dp", "mp"), None),
        P(("dp", "mp"), None),
        P(("dp", "mp"), None),
        P("mp", "dp"),
        P("mp", "dp"),
    )
    return jax.shard_map(shards, mesh=mesh, in_specs=in_specs, out_specs=out_specs, check_vma=False)
```

```python
import functools
import math

import jax
import jax.numpy as jnp
from jax import lax
from jax.experimental import pallas as pl
from jax.experimental.pallas import tpu as pltpu
from jax.sharding import PartitionSpec as P

NZ, NY, NC, NX = 8, 4, 2, 4
POOL = NY * NX
ROWS = 64
WIDE = POOL * ROWS
HD = 128
NH = 3
SLOTS = 512
HALF = SLOTS // NC
PART = HALF // NZ
FEATURES = 6144
EPSILON = 1e-06
MESH = pl.DeviceIdType.MESH
BF = jnp.bfloat16
F32 = jnp.float32
OUTWARD = 5
BACKWARD = 6
BEHIND = 3
VMEM_LIMIT = 60 * 1024 * 1024


def iota(shape, dim):
    return lax.broadcasted_iota(jnp.int32, shape, dim)


def dot(a, b, ca=1, cb=0):
    return lax.dot_general(a, b, (((ca,), (cb,)), ((), ())), preferred_element_type=F32)


def onehot(flags):
    return jnp.where(flags, 1.0, 0.0).astype(BF)


def coords():
    dp = lax.axis_index("dp")
    return (lax.div(dp, 8), lax.rem(lax.div(dp, 2), 4), lax.rem(dp, 2), lax.axis_index("mp"))


def device(z, y, c, x):
    return ((z * NY + y) * NC + c, x)


def build_place(cap, z, c, codes, place, tri):
    lower, upper = iota((WIDE, WIDE), 0), iota((WIDE, WIDE), 1)
    earlier = lower < upper
    tri[...] = onehot(earlier)
    own = codes[pl.ds(z * NC + c, 1), :]
    own_plane = own >> 6
    planes = own_plane == iota((NZ, WIDE), 0)
    mine = jnp.concatenate([codes[pl.ds(u * NC + c, 1), :] for u in range(NZ)], axis=0)
    members = (mine >> 6) == z
    both = jnp.concatenate([onehot(planes), onehot(members)], axis=0)
    before = dot(both, tri[...])
    own_rank = jnp.sum(jnp.where(planes, before[:NZ], 0.0), axis=0, keepdims=True)
    position = own_rank.astype(jnp.int32) + own_plane * cap
    for step in range(NZ):
        place[pl.ds(step * cap, cap), :] = onehot(position == iota((cap, WIDE), 0) + step * cap)
    return position, jnp.where(members, before[NZ:], -1.0).astype(jnp.int32)


def build_expand(cap, z, c, position, message_rank, codes, turned, expand, lab_col, lab_row, tri):
    column = jnp.broadcast_to(position.astype(F32), (HD, WIDE)).T
    for k in range(0, NZ * cap, HD):
        turned[:, k : k + HD] = onehot(column == (iota((WIDE, HD), 1) + k).astype(F32))
    lane = iota((1, WIDE), 1)
    lower, upper = iota((WIDE, WIDE), 0), iota((WIDE, WIDE), 1)
    earlier = lower < upper
    tri[...] = onehot(earlier & ((lower >> 6) == (upper >> 6)))
    source = (lane >> 6) * 2
    for u in range(NZ):
        for k in range(NC):
            core = c if k == 0 else 1 - c
            row = codes[pl.ds(u * NC + core, 1), :]
            group = iota((NZ, WIDE), 0)
            name = z * 8 + (group & 3) * 2 + jnp.where(group < NY, c, 1 - c)
            member = (row >> 3) == name
            count = dot(onehot(member), tri[...])
            slot = jnp.where(member, count + source.astype(F32), -1.0)
            groups = NZ if k == 0 else NY
            blocks = [slot[g : g + 1, :].astype(jnp.int32) == iota((PART, WIDE), 0) for g in range(groups)]
            chosen = onehot(jnp.concatenate(blocks, axis=0))
            image = jnp.broadcast_to(((row & 7) + 1).astype(F32), (HD, WIDE)).astype(BF)
            label = dot(chosen[: NY * PART], image, 1, 1)
            for g in range(NY):
                at = pl.multiple_of(core * HALF + u * PART, PART)
                found = label[g * PART : (g + 1) * PART]
                empty = -1.0 - (at + iota((PART, HD), 0)).astype(F32)
                lab_col[g, pl.ds(at, PART), :] = jnp.where(found > 0.5, found, empty)
            if k == 0:
                ranks = onehot(message_rank[u : u + 1, :] == iota((cap, WIDE), 0))
                expand[u] = dot(chosen, ranks, 1, 1).astype(BF)
    for g in range(NY):
        lab_row[g] = lab_col[g].T[:8]


def normalize(block):
    floats = block.astype(F32)
    average = jnp.mean(floats, axis=-1, keepdims=True)
    centred = floats - average
    inverse = lax.rsqrt(jnp.mean(centred * centred, axis=-1, keepdims=True) + EPSILON)
    return centred * inverse, inverse


def norm_back(grad_hat, normed, inverse):
    first = jnp.mean(grad_hat, axis=-1, keepdims=True)
    second = jnp.mean(grad_hat * normed, axis=-1, keepdims=True)
    return inverse * (grad_hat - first - normed * second)


def head_pass(query, key, value, cot, gain_q, gain_k, col, row, width=256):
    scale = 1.0 / math.sqrt(HD)
    query_hat, query_inverse = normalize(query)
    key_hat, key_inverse = normalize(key)
    query_low = (query_hat * gain_q).astype(BF)
    key_low = (key_hat * gain_k).astype(BF)
    col = jnp.concatenate([col] * (width // HD), axis=1)
    outs, grads_q = [], []
    grad_v = jnp.zeros((SLOTS, HD), F32)
    grad_k = jnp.zeros((SLOTS, HD), F32)
    for at in range(0, SLOTS, width):
        q = query_low[at : at + width]
        g = cot[at : at + width]
        scores = dot(key_low, q, 1, 1)
        scores = jnp.where(col == row[:, at : at + width], scores, -1e30)
        top = jnp.max(scores, axis=0, keepdims=True)
        weights = jnp.exp((scores - top) * scale)
        attention = weights * (1.0 / jnp.sum(weights, axis=0, keepdims=True))
        low = attention.astype(BF)
        probs = dot(value, g, 1, 1)
        inner = jnp.sum(attention * probs, axis=0, keepdims=True)
        grad_s = (attention * (probs - inner) * scale).astype(BF)
        outs.append(dot(low, value, 0, 0))
        grads_q.append(dot(grad_s, key_low, 0, 0))
        grad_v = grad_v + dot(low, g)
        grad_k = grad_k + dot(grad_s, q)
    grad_q = jnp.concatenate(grads_q, axis=0)
    term_q = jnp.sum(grad_q * query_hat, axis=0, keepdims=True)
    term_k = jnp.sum(grad_k * key_hat, axis=0, keepdims=True)
    back_q = norm_back(grad_q * gain_q, query_hat, query_inverse)
    back_k = norm_back(grad_k * gain_k, key_hat, key_inverse)
    packed = jnp.concatenate(
        [jnp.concatenate(outs, axis=0).astype(BF), back_q.astype(BF), back_k.astype(BF), grad_v.astype(BF)],
        axis=1,
    )
    return packed, term_q, term_k


def main_kernel(
    cap, query_in, key_in, value_in, grad_in, gain_q, gain_k, codes, out, gain_out,
    rows, grads, xin, gob, zin, half_out, packed, res, rin, zro, zri,
    place, turned, expand, lab_col, lab_row, tri, shuffle, gacc, gz, gs, gm, gt, gy,
    load_sem, own_sem, grad_own, out_own, xs, xr, gos, gor, zs, zr, hs, hr, rs, rr, zrs, zrr, us, ur,
    gzs, gzr, gms, gmr, gys, gyr,
):
    uout = xin
    zout = zro
    z, y, c, x = coords()
    spot = y * NX + x
    loads = [
        pltpu.make_async_copy(ref, rows.at[k], load_sem.at[k])
        for k, ref in enumerate((query_in, key_in, value_in))
    ]
    loads.append(pltpu.make_async_copy(grad_in, grads, load_sem.at[3]))
    for load in loads:
        load.start()

    barrier = pltpu.get_barrier_semaphore()

    def greet(target):
        pl.semaphore_signal(barrier, inc=1, device_id=target, device_id_type=MESH)

    def xy_peer(i):
        return lax.rem(y + lax.div(i, NX), NY), lax.rem(x + lax.rem(i, NX), NX)

    def each(low, high, body):
        def step(i, carry):
            body(i)
            return carry

        lax.fori_loop(low, high, step, 0)

    def greet_xy(i):
        py, px = xy_peer(i)
        greet(device(z, py, c, px))

    def greet_z(d):
        greet(device(lax.rem(z + d, NZ), y, c, x))

    each(1, POOL, greet_xy)
    each(1, NZ, greet_z)
    mate = device(z, y, 1 - c, x)
    greet(mate)
    pl.semaphore_wait(barrier, POOL - 1 + NZ - 1 + 1)

    def remote(src, dst, send, recv, target):
        return pltpu.make_async_remote_copy(
            src_ref=src, dst_ref=dst, send_sem=send, recv_sem=recv, device_id=target, device_id_type=MESH
        )

    def columns(py, px, h):
        return pl.ds(pl.multiple_of(px * 1536 + py * 384 + h * HD, HD), HD)

    def piece(h, a):
        return a if isinstance(h, int) and h == 0 else h + 2

    def xy_start(h, a, n):
        f = piece(h, a)

        def start(i):
            py, px = xy_peer(i)
            remote(
                rows.at[pl.ds(a, n), :, columns(py, px, h)], xin.at[h, pl.ds(a, n), spot],
                xs.at[f], xr.at[f], device(z, py, c, px),
            ).start()

        each(1, POOL, start)
        xy_own(h, a, n).start()

    def xy_own(h, a, n):
        return pltpu.make_async_copy(
            rows.at[pl.ds(a, n), :, columns(y, x, h)], xin.at[h, pl.ds(a, n), spot], own_sem.at[piece(h, a)]
        )

    def xy_all(h, a, n):
        f = piece(h, a)
        area = xin.at[h, pl.ds(a, n), 0 : POOL - 1]
        return remote(area, area, xs.at[f], xr.at[f], mate)

    def xy_arrive(h, a, n):
        xy_all(h, a, n).wait_recv()
        xy_own(h, a, n).wait()

    def grad_columns(py, h):
        return pl.ds(pl.multiple_of(py * 384 + h * HD, HD), HD)

    def grad_copy(h, d):
        py = lax.rem(y + d, NY)
        return remote(grads.at[:, grad_columns(py, h)], gob.at[h, y], gos.at[h, d], gor.at[h, d], device(z, py, c, x))

    def grad_arrival(h, d):
        py = lax.rem(y + NY - d, NY)
        return remote(grads.at[:, grad_columns(y, h)], gob.at[h, py], gos.at[h, d], gor.at[h, d], device(z, py, c, x))

    def grad_keep(h):
        return pltpu.make_async_copy(grads.at[:, grad_columns(y, h)], gob.at[h, y], grad_own.at[h])

    def send_grads(h):
        each(1, NY, lambda d: grad_copy(h, d).start())
        grad_keep(h).start()

    for k in range(3):
        loads[k].wait()
        xy_start(0, k, 1)
    loads[3].wait()
    position, message_rank = build_place(cap, z, c, codes, place, tri)
    slot = iota((SLOTS, SLOTS), 0)
    pool = (slot >> 1) & 15
    canon = (pool & 3) * 128 + ((slot >> 5) & 7) * 16 + (pool >> 2) * 4 + (slot >> 8) * 2 + (slot & 1)
    shuffle[...] = onehot(canon == iota((SLOTS, SLOTS), 1))
    gacc[...] = jnp.zeros_like(gacc)

    def z_all(h):
        area = zout.at[h, 0 : NZ - 1, :, 0 : 3 * HD]
        return remote(area, area, zs.at[h], zr.at[h, 0], mate)

    def z_arrival(h, d):
        area = zin.at[h, lax.rem(z + NZ - d, NZ)]
        return remote(area, area, zs.at[h], zr.at[h, d], mate)

    def compact(h, a, n):
        part = slice(a * HD, (a + n) * HD)

        def message(pz):
            if n == 1:
                pooled = xin[h, a].reshape(WIDE, HD)
            else:
                pooled = jnp.concatenate([xin[h, k].reshape(WIDE, HD) for k in range(n)], axis=1)
            chosen = place[pl.ds(pl.multiple_of(pz * cap, 16), cap), :]
            return dot(chosen, pooled).astype(BF)

        def to_plane(d):
            pz = lax.rem(z + d, NZ)
            found = message(pz)

            @pl.when(d < NZ)
            def _():
                zout[h, pz, :, part] = found
                remote(
                    zout.at[h, pz, :, part], zin.at[h, z, :, part], zs.at[h], zr.at[h, d], device(pz, y, c, x)
                ).start()

            @pl.when(d == NZ)
            def _():
                zin[h, z, :, part] = found

        each(1, NZ + 1, to_plane)

    def first_head(a):
        xy_arrive(0, a, 1)
        if a == 1:
            xy_start(1, 0, 3)
        if a == 2:
            send_grads(0)
        compact(0, a, 1)

    for a in range(3):
        first_head(a)
    build_expand(cap, z, c, position, message_rank, codes, turned, expand, lab_col, lab_row, tri)

    def other_head(h):
        xy_arrive(h, 0, 3)

        @pl.when(h == 1)
        def _():
            xy_start(2, 0, 3)

        send_grads(h)
        compact(h, 0, 3)

    each(1, NH, other_head)

    def half_copy(h):
        return remote(half_out, packed.at[h, :, c], hs.at[h], hr.at[h], mate)

    def half_arrival(h):
        return remote(half_out, packed.at[h, :, 1 - c], hs.at[h], hr.at[h], mate)

    def res_copy(h):
        return remote(res.at[1 - c], rin, rs.at[h], rr.at[h], mate)

    def work(h):
        def unfold(d):
            pz = lax.rem(z + NZ - d, NZ)

            @pl.when(d > 0)
            def _():
                z_arrival(h, d).wait_recv()

            spread = dot(expand[pz], zin[h, pz]).astype(BF)
            at = pl.ds(pl.multiple_of(pz * PART, PART), PART)
            for g in range(NY):
                packed[h, g, c, at, :] = spread[g * PART : (g + 1) * PART]
                half_out[g, at, :] = spread[(NY + g) * PART : (NY + g + 1) * PART]

        each(0, NZ, unfold)
        half_copy(h).start()
        each(1, NY, lambda d: grad_arrival(h, d).wait_recv())
        grad_keep(h).wait()
        half_arrival(h).wait_recv()

        head = y * NH + h
        own_gain_q = gain_q[pl.ds(head, 1), :]
        own_gain_k = gain_k[pl.ds(head, 1), :]

        def group(g):
            block = packed[h, g].reshape(SLOTS, 3 * HD)
            col = lab_col[g]
            cot = dot(shuffle[...], gob[h, g])
            cot = jnp.where(col > 0.0, cot, 0.0).astype(BF)
            result, term_q, term_k = head_pass(
                block[:, :HD], block[:, HD : 2 * HD], block[:, 2 * HD :], cot,
                own_gain_q, own_gain_k, col, lab_row[g, 0:1, :],
            )
            res[0, g] = result[:HALF]
            res[1, g] = result[HALF:]
            gacc[h, 0:1, :] += term_q
            gacc[h, 1:2, :] += term_k

        each(0, NY, group)
        res_copy(h).start()
        res_copy(h).wait()
        half_copy(h).wait_send()
        z_all(h).wait_send()

    def back_all(b):
        area = zri.at[0, 0 : NZ - 1, :, 0 : 2 * HD]
        return remote(area, area, zrs.at[b], zrr.at[b], mate)

    def send_back(h, half):
        b = h * 2 + half
        part = slice(half * 2 * HD, (half + 1) * 2 * HD)

        def fold(d):
            pz = lax.rem(z + d, NZ)
            at = pl.ds(pl.multiple_of(pz * PART, PART), PART)
            blocks = [res[c, g, at, part] for g in range(NY)] + [rin[g, at, part] for g in range(NY)]
            folded = dot(expand[pz], jnp.concatenate(blocks, axis=0), 0, 0).astype(BF)

            @pl.when(d < NZ)
            def _():
                zro[h, pz, :, part] = folded
                remote(
                    zro.at[h, pz, :, part], zri.at[h, z, :, part], zrs.at[b], zrr.at[b], device(pz, y, c, x)
                ).start()

            @pl.when(d == NZ)
            def _():
                zri[h, z, :, part] = folded

        each(1, NZ + 1, fold)

    def u_own(b):
        h = lax.div(b, 2)
        two = pl.ds(lax.rem(b, 2) * 2, 2)
        return pltpu.make_async_copy(uout.at[h, two, spot], out.at[two, :, columns(y, x, h)], out_own.at[b])

    def u_all(b):
        area = out.at[0:2, :, 0 : (POOL - 1) * HD]
        return remote(area, area, us.at[b], ur.at[b], mate)

    def unpool(h, half):
        b = h * 2 + half
        first = half * 2
        part = slice(first * HD, (first + 2) * HD)
        back_all(b).wait_recv()

        def block(k):
            chosen = turned[pl.ds(pl.multiple_of(k * 4 * ROWS, 4 * ROWS), 4 * ROWS), :]
            found = dot(chosen, zri[h, :, :, part].reshape(NZ * cap, 2 * HD)).astype(BF)
            for r in range(4):
                for m in range(2):
                    uout[h, first + m, k * 4 + r] = found[r * ROWS : (r + 1) * ROWS, m * HD : (m + 1) * HD]

        each(0, POOL // 4, block)

        def start(i):
            py, px = xy_peer(i)
            two = pl.ds(first, 2)
            remote(
                uout.at[h, two, py * NX + px], out.at[two, :, columns(y, x, h)],
                us.at[b], ur.at[b], device(z, py, c, px),
            ).start()

        each(1, POOL, start)
        u_own(b).start()

    def gz_copy(d):
        return remote(gacc, gz.at[z], gzs.at[d], gzr.at[d], device(lax.rem(z + d, NZ), y, c, x))

    def gz_arrival(d):
        pz = lax.rem(z + NZ - d, NZ)
        return remote(gacc, gz.at[pz], gzs.at[d], gzr.at[d], device(pz, y, c, x))

    def gm_copy():
        return remote(gs, gm, gms, gmr, mate)

    def gy_copy(d):
        return remote(gt, gy.at[y], gys.at[d], gyr.at[d], device(z, lax.rem(y + d, NY), c, x))

    def gy_arrival(d):
        py = lax.rem(y + NY - d, NY)
        return remote(gt, gy.at[py], gys.at[d], gyr.at[d], device(z, py, c, x))

    def back(h, half):
        b = h * 2 + half
        if half == 0:

            @pl.when(b < BACKWARD)
            def _():
                work(h)

        @pl.when((b >= BEHIND) & (b < BACKWARD + BEHIND))
        def _():
            back_all(b - BEHIND).wait_send()

        @pl.when(b < BACKWARD)
        def _():
            send_back(h, half)

        @pl.when(b == BACKWARD - 1)
        def _():
            each(1, NZ, lambda d: gz_copy(d).start())
            gz[z] = gacc[...]

        @pl.when(b == BACKWARD)
        def _():
            each(1, NZ, lambda d: gz_arrival(d).wait_recv())
            gs[...] = jnp.sum(gz[...], axis=0)
            gm_copy().start()
            for f in range(3):
                xy_all(0, f, 1).wait_send()
            for h in range(1, NH):
                xy_all(h, 0, 3).wait_send()
            each(0, NH, lambda h: each(1, NY, lambda d: grad_copy(h, d).wait_send()))

        @pl.when(b == BACKWARD + 1)
        def _():
            gm_copy().wait_recv()
            gt[...] = gs[...] + gm[...]
            each(1, NY, lambda d: gy_copy(d).start())
            gy[y] = gt[...]

        @pl.when(b == BACKWARD + 2)
        def _():
            each(1, NY, lambda d: gy_arrival(d).wait_recv())
            gain_out[...] = gy[...]
            each(1, NZ, lambda d: gz_copy(d).wait_send())
            gm_copy().wait_send()
            each(1, NY, lambda d: gy_copy(d).wait_send())

        @pl.when((b >= BEHIND) & (b < BACKWARD + BEHIND))
        def _():
            unpool(h + (half - BEHIND) // 2, (half - BEHIND) % 2)

    def both(h):
        for half in range(2):
            back(h, half)

    each(0, (BACKWARD + BEHIND + 1) // 2, both)

    def finish(b):
        u_all(b).wait()
        u_own(b).wait()

    each(0, BACKWARD, finish)


def exchange(cap, collective_id, *operands):
    vmem = pltpu.VMEM
    dma = pltpu.SemaphoreType.DMA
    any_spec = pl.BlockSpec(memory_space=pl.ANY)
    vmem_spec = pl.BlockSpec(memory_space=pltpu.VMEM)
    scratch = [
        vmem((3, ROWS, FEATURES), BF),
        vmem((SLOTS, 1536), BF),
        vmem((NH, 4, POOL, ROWS, HD), BF),
        vmem((NH, NY, SLOTS, HD), BF),
        vmem((NH, NZ, cap, 3 * HD), BF),
        vmem((NY, HALF, 3 * HD), BF),
        vmem((NH, NY, NC, HALF, 3 * HD), BF),
        vmem((NC, NY, HALF, 4 * HD), BF),
        vmem((NY, HALF, 4 * HD), BF),
        vmem((NH, NZ, cap, 4 * HD), BF),
        vmem((NH, NZ, cap, 4 * HD), BF),
        vmem((NZ * cap, WIDE), BF),
        vmem((WIDE, NZ * cap), BF),
        vmem((NZ, 2 * NY * PART, cap), BF),
        vmem((NY, SLOTS, HD), F32),
        vmem((NY, 8, SLOTS), F32),
        vmem((WIDE, WIDE), BF),
        vmem((SLOTS, SLOTS), BF),
        vmem((NH, 8, HD), F32),
        vmem((NZ, NH, 8, HD), F32),
        vmem((NH, 8, HD), F32),
        vmem((NH, 8, HD), F32),
        vmem((NH, 8, HD), F32),
        vmem((NY, NH, 8, HD), F32),
        dma((4,)),
        dma((OUTWARD,)),
        dma((NH,)),
        dma((BACKWARD,)),
        dma((OUTWARD,)),
        dma((OUTWARD,)),
        dma((NH, NY)),
        dma((NH, NY)),
        dma((NH,)),
        dma((NH, NZ)),
    ]
    scratch += [dma((NH,)), dma((NH,)), dma((NH,)), dma((NH,))]
    scratch += [dma((BACKWARD,)), dma((BACKWARD,)), dma((BACKWARD,)), dma((BACKWARD,))]
    scratch += [dma((NZ,)), dma((NZ,)), dma(()), dma(()), dma((NY,)), dma((NY,))]
    return pl.pallas_call(
        functools.partial(main_kernel, cap),
        name=f"exchange_{cap}",
        out_shape=(
            jax.ShapeDtypeStruct((4, ROWS, FEATURES), BF),
            jax.ShapeDtypeStruct((NY, NH, 8, HD), F32),
        ),
        in_specs=[any_spec] * 4 + [vmem_spec] * 3,
        out_specs=(any_spec, vmem_spec),
        scratch_shapes=scratch,
        compiler_params=pltpu.CompilerParams(
            collective_id=collective_id, has_side_effects=True, vmem_limit_bytes=VMEM_LIMIT
        ),
    )(*operands)


ROOMS = (160, 176, POOL * NY * NC * 2)


def shards(
    query_rows, key_rows, value_rows, destination, image_slot, gain_query, gain_key, grad_output
):
    codes = (destination * 8 + image_slot).reshape(NZ, NY, NC, NX, ROWS)
    codes = codes.transpose(0, 2, 1, 3, 4).reshape(NZ * NC, WIDE)
    operands = (query_rows, key_rows, value_rows, grad_output, gain_query, gain_key, codes)
    planes = codes[:, None, :] >> 6 == jnp.arange(NZ, dtype=jnp.int32)[None, :, None]
    most = jnp.max(jnp.sum(planes.astype(jnp.int32), axis=-1))
    level = sum((most > room).astype(jnp.int32) for room in ROOMS[:-1])
    branches = [functools.partial(exchange, room, k) for k, room in enumerate(ROOMS)]
    out, gains = lax.switch(level, branches, *operands)
    first = lax.axis_index("dp") * 2
    gains = lax.dynamic_slice_in_dim(gains, first, 2, axis=3)
    grad_gain_query = gains[:, :, 0].reshape(NY * NH, 2)
    grad_gain_key = gains[:, :, 1].reshape(NY * NH, 2)
    return (out[0], out[1], out[2], out[3], grad_gain_query, grad_gain_key)


def solution(mesh):
    in_specs = (
        P(("dp", "mp"), None),
        P(("dp", "mp"), None),
        P(("dp", "mp"), None),
        P(),
        P(),
        P("mp", None),
        P("mp", None),
        P("dp", "mp"),
    )
    out_specs = (
        P(("dp", "mp"), None),
        P(("dp", "mp"), None),
        P(("dp", "mp"), None),
        P(("dp", "mp"), None),
        P("mp", "dp"),
        P("mp", "dp"),
    )
    return jax.shard_map(shards, mesh=mesh, in_specs=in_specs, out_specs=out_specs, check_vma=False)
```

```python
import functools
import math

import jax
import jax.numpy as jnp
from jax import lax
from jax.experimental import pallas as pl
from jax.experimental.pallas import tpu as pltpu
from jax.sharding import PartitionSpec as P

NZ, NY, NC, NX = 8, 4, 2, 4
POOL = NY * NX
ROWS = 64
WIDE = POOL * ROWS
HD = 128
NH = 3
SLOTS = 512
HALF = SLOTS // NC
PART = HALF // NZ
FEATURES = 6144
EPSILON = 1e-06
MESH = pl.DeviceIdType.MESH
BF = jnp.bfloat16
F32 = jnp.float32
OUTWARD = 5
BACKWARD = 6
BEHIND = 2
VMEM_LIMIT = 60 * 1024 * 1024


def iota(shape, dim):
    return lax.broadcasted_iota(jnp.int32, shape, dim)


def dot(a, b, ca=1, cb=0):
    return lax.dot_general(a, b, (((ca,), (cb,)), ((), ())), preferred_element_type=F32)


def onehot(flags):
    return jnp.where(flags, 1.0, 0.0).astype(BF)


def coords():
    dp = lax.axis_index("dp")
    return (lax.div(dp, 8), lax.rem(lax.div(dp, 2), 4), lax.rem(dp, 2), lax.axis_index("mp"))


def device(z, y, c, x):
    return ((z * NY + y) * NC + c, x)


def build_place(cap, z, c, codes, place, tri):
    lower, upper = iota((WIDE, WIDE), 0), iota((WIDE, WIDE), 1)
    earlier = lower < upper
    tri[...] = onehot(earlier)
    own = codes[pl.ds(z * NC + c, 1), :]
    own_plane = own >> 6
    planes = own_plane == iota((NZ, WIDE), 0)
    mine = jnp.concatenate([codes[pl.ds(u * NC + c, 1), :] for u in range(NZ)], axis=0)
    members = (mine >> 6) == z
    both = jnp.concatenate([onehot(planes), onehot(members)], axis=0)
    before = dot(both, tri[...])
    own_rank = jnp.sum(jnp.where(planes, before[:NZ], 0.0), axis=0, keepdims=True)
    position = own_rank.astype(jnp.int32) + own_plane * cap
    for step in range(NZ):
        place[pl.ds(step * cap, cap), :] = onehot(position == iota((cap, WIDE), 0) + step * cap)
    return position, jnp.where(members, before[NZ:], -1.0).astype(jnp.int32)


def build_expand(cap, z, c, position, message_rank, codes, turned, expand, lab_col, lab_row, tri):
    column = jnp.broadcast_to(position.astype(F32), (HD, WIDE)).T
    for k in range(0, NZ * cap, HD):
        turned[:, k : k + HD] = onehot(column == (iota((WIDE, HD), 1) + k).astype(F32))
    lane = iota((1, WIDE), 1)
    lower, upper = iota((WIDE, WIDE), 0), iota((WIDE, WIDE), 1)
    earlier = lower < upper
    tri[...] = onehot(earlier & ((lower >> 6) == (upper >> 6)))
    source = (lane >> 6) * 2
    for u in range(NZ):
        for k in range(NC):
            core = c if k == 0 else 1 - c
            row = codes[pl.ds(u * NC + core, 1), :]
            group = iota((NZ, WIDE), 0)
            name = z * 8 + (group & 3) * 2 + jnp.where(group < NY, c, 1 - c)
            member = (row >> 3) == name
            count = dot(onehot(member), tri[...])
            slot = jnp.where(member, count + source.astype(F32), -1.0)
            groups = NZ if k == 0 else NY
            blocks = [slot[g : g + 1, :].astype(jnp.int32) == iota((PART, WIDE), 0) for g in range(groups)]
            chosen = onehot(jnp.concatenate(blocks, axis=0))
            image = jnp.broadcast_to(((row & 7) + 1).astype(F32), (HD, WIDE)).astype(BF)
            label = dot(chosen[: NY * PART], image, 1, 1)
            for g in range(NY):
                at = pl.multiple_of(core * HALF + u * PART, PART)
                found = label[g * PART : (g + 1) * PART]
                empty = -1.0 - (at + iota((PART, HD), 0)).astype(F32)
                lab_col[g, pl.ds(at, PART), :] = jnp.where(found > 0.5, found, empty)
            if k == 0:
                ranks = onehot(message_rank[u : u + 1, :] == iota((cap, WIDE), 0))
                expand[u] = dot(chosen, ranks, 1, 1).astype(BF)
    for g in range(NY):
        lab_row[g] = lab_col[g].T[:8]


def normalize(block):
    floats = block.astype(F32)
    average = jnp.mean(floats, axis=-1, keepdims=True)
    centred = floats - average
    inverse = lax.rsqrt(jnp.mean(centred * centred, axis=-1, keepdims=True) + EPSILON)
    return centred * inverse, inverse


def norm_back(grad_hat, normed, inverse):
    first = jnp.mean(grad_hat, axis=-1, keepdims=True)
    second = jnp.mean(grad_hat * normed, axis=-1, keepdims=True)
    return inverse * (grad_hat - first - normed * second)


def head_pass(query, key, value, cot, gain_q, gain_k, col, row, width=256):
    scale = 1.0 / math.sqrt(HD)
    query_hat, query_inverse = normalize(query)
    key_hat, key_inverse = normalize(key)
    query_low = (query_hat * gain_q).astype(BF)
    key_low = (key_hat * gain_k).astype(BF)
    col = jnp.concatenate([col] * (width // HD), axis=1)
    outs, grads_q = [], []
    grad_v = jnp.zeros((SLOTS, HD), F32)
    grad_k = jnp.zeros((SLOTS, HD), F32)
    for at in range(0, SLOTS, width):
        q = query_low[at : at + width]
        g = cot[at : at + width]
        scores = dot(key_low, q, 1, 1)
        scores = jnp.where(col == row[:, at : at + width], scores, -1e30)
        top = jnp.max(scores, axis=0, keepdims=True)
        weights = jnp.exp((scores - top) * scale)
        attention = weights * (1.0 / jnp.sum(weights, axis=0, keepdims=True))
        low = attention.astype(BF)
        probs = dot(value, g, 1, 1)
        inner = jnp.sum(attention * probs, axis=0, keepdims=True)
        grad_s = (attention * (probs - inner) * scale).astype(BF)
        outs.append(dot(low, value, 0, 0))
        grads_q.append(dot(grad_s, key_low, 0, 0))
        grad_v = grad_v + dot(low, g)
        grad_k = grad_k + dot(grad_s, q)
    grad_q = jnp.concatenate(grads_q, axis=0)
    term_q = jnp.sum(grad_q * query_hat, axis=0, keepdims=True)
    term_k = jnp.sum(grad_k * key_hat, axis=0, keepdims=True)
    back_q = norm_back(grad_q * gain_q, query_hat, query_inverse)
    back_k = norm_back(grad_k * gain_k, key_hat, key_inverse)
    packed = jnp.concatenate(
        [jnp.concatenate(outs, axis=0).astype(BF), back_q.astype(BF), back_k.astype(BF), grad_v.astype(BF)],
        axis=1,
    )
    return packed, term_q, term_k


def main_kernel(
    cap, query_in, key_in, value_in, grad_in, gain_q, gain_k, codes, out, gain_out,
    rows, grads, xin, gob, zin, half_out, packed, res, rin, zro, zri,
    place, turned, expand, lab_col, lab_row, tri, shuffle, gacc, gz, gs, gm, gt, gy,
    load_sem, own_sem, grad_own, out_own, xs, xr, gos, gor, zs, zr, hs, hr, rs, rr, zrs, zrr, us, ur,
    gzs, gzr, gms, gmr, gys, gyr,
):
    uout = xin
    zout = zro
    z, y, c, x = coords()
    spot = y * NX + x
    loads = [
        pltpu.make_async_copy(ref, rows.at[k], load_sem.at[k])
        for k, ref in enumerate((query_in, key_in, value_in))
    ]
    loads.append(pltpu.make_async_copy(grad_in, grads, load_sem.at[3]))
    for load in loads:
        load.start()

    barrier = pltpu.get_barrier_semaphore()

    def greet(target):
        pl.semaphore_signal(barrier, inc=1, device_id=target, device_id_type=MESH)

    def xy_peer(i):
        return lax.rem(y + lax.div(i, NX), NY), lax.rem(x + lax.rem(i, NX), NX)

    def each(low, high, body):
        def step(i, carry):
            body(i)
            return carry

        lax.fori_loop(low, high, step, 0)

    def greet_xy(i):
        py, px = xy_peer(i)
        greet(device(z, py, c, px))

    def greet_z(d):
        greet(device(lax.rem(z + d, NZ), y, c, x))

    each(1, POOL, greet_xy)
    each(1, NZ, greet_z)
    mate = device(z, y, 1 - c, x)
    greet(mate)
    pl.semaphore_wait(barrier, POOL - 1 + NZ - 1 + 1)

    def remote(src, dst, send, recv, target):
        return pltpu.make_async_remote_copy(
            src_ref=src, dst_ref=dst, send_sem=send, recv_sem=recv, device_id=target, device_id_type=MESH
        )

    def columns(py, px, h):
        return pl.ds(pl.multiple_of(px * 1536 + py * 384 + h * HD, HD), HD)

    def piece(h, a):
        return a if isinstance(h, int) and h == 0 else h + 2

    def xy_start(h, a, n):
        f = piece(h, a)

        def start(i):
            py, px = xy_peer(i)
            remote(
                rows.at[pl.ds(a, n), :, columns(py, px, h)], xin.at[h, pl.ds(a, n), spot],
                xs.at[f], xr.at[f], device(z, py, c, px),
            ).start()

        each(1, POOL, start)
        xy_own(h, a, n).start()

    def xy_own(h, a, n):
        return pltpu.make_async_copy(
            rows.at[pl.ds(a, n), :, columns(y, x, h)], xin.at[h, pl.ds(a, n), spot], own_sem.at[piece(h, a)]
        )

    def xy_all(h, a, n):
        f = piece(h, a)
        area = xin.at[h, pl.ds(a, n), 0 : POOL - 1]
        return remote(area, area, xs.at[f], xr.at[f], mate)

    def xy_arrive(h, a, n):
        xy_all(h, a, n).wait_recv()
        xy_own(h, a, n).wait()

    def grad_columns(py, h):
        return pl.ds(pl.multiple_of(py * 384 + h * HD, HD), HD)

    def grad_copy(h, d):
        py = lax.rem(y + d, NY)
        return remote(grads.at[:, grad_columns(py, h)], gob.at[h, y], gos.at[h, d], gor.at[h, d], device(z, py, c, x))

    def grad_arrival(h, d):
        py = lax.rem(y + NY - d, NY)
        return remote(grads.at[:, grad_columns(y, h)], gob.at[h, py], gos.at[h, d], gor.at[h, d], device(z, py, c, x))

    def grad_keep(h):
        return pltpu.make_async_copy(grads.at[:, grad_columns(y, h)], gob.at[h, y], grad_own.at[h])

    def send_grads(h):
        each(1, NY, lambda d: grad_copy(h, d).start())
        grad_keep(h).start()

    for k in range(3):
        loads[k].wait()
        xy_start(0, k, 1)
    loads[3].wait()
    position, message_rank = build_place(cap, z, c, codes, place, tri)
    slot = iota((SLOTS, SLOTS), 0)
    pool = (slot >> 1) & 15
    canon = (pool & 3) * 128 + ((slot >> 5) & 7) * 16 + (pool >> 2) * 4 + (slot >> 8) * 2 + (slot & 1)
    shuffle[...] = onehot(canon == iota((SLOTS, SLOTS), 1))
    gacc[...] = jnp.zeros_like(gacc)

    def z_all(h):
        area = zout.at[h, 0 : NZ - 1, :, 0 : 3 * HD]
        return remote(area, area, zs.at[h], zr.at[h, 0], mate)

    def z_arrival(h, d):
        area = zin.at[h, lax.rem(z + NZ - d, NZ)]
        return remote(area, area, zs.at[h], zr.at[h, d], mate)

    def compact(h, a, n):
        part = slice(a * HD, (a + n) * HD)

        def message(pz):
            if n == 1:
                pooled = xin[h, a].reshape(WIDE, HD)
            else:
                pooled = jnp.concatenate([xin[h, k].reshape(WIDE, HD) for k in range(n)], axis=1)
            chosen = place[pl.ds(pl.multiple_of(pz * cap, 16), cap), :]
            return dot(chosen, pooled).astype(BF)

        def to_plane(d):
            pz = lax.rem(z + d, NZ)
            found = message(pz)

            @pl.when(d < NZ)
            def _():
                zout[h, pz, :, part] = found
                remote(
                    zout.at[h, pz, :, part], zin.at[h, z, :, part], zs.at[h], zr.at[h, d], device(pz, y, c, x)
                ).start()

            @pl.when(d == NZ)
            def _():
                zin[h, z, :, part] = found

        each(1, NZ + 1, to_plane)

    def first_head(a):
        xy_arrive(0, a, 1)
        if a == 1:
            xy_start(1, 0, 3)
        if a == 2:
            send_grads(0)
        compact(0, a, 1)

    for a in range(3):
        first_head(a)
    build_expand(cap, z, c, position, message_rank, codes, turned, expand, lab_col, lab_row, tri)

    def other_head(h):
        xy_arrive(h, 0, 3)

        @pl.when(h == 1)
        def _():
            xy_start(2, 0, 3)

        send_grads(h)
        compact(h, 0, 3)

    each(1, NH, other_head)

    def half_copy(h):
        return remote(half_out, packed.at[h, :, c], hs.at[h], hr.at[h], mate)

    def half_arrival(h):
        return remote(half_out, packed.at[h, :, 1 - c], hs.at[h], hr.at[h], mate)

    def res_copy(h):
        return remote(res.at[1 - c], rin, rs.at[h], rr.at[h], mate)

    def work(h):
        def unfold(d):
            pz = lax.rem(z + NZ - d, NZ)

            @pl.when(d > 0)
            def _():
                z_arrival(h, d).wait_recv()

            spread = dot(expand[pz], zin[h, pz]).astype(BF)
            at = pl.ds(pl.multiple_of(pz * PART, PART), PART)
            for g in range(NY):
                packed[h, g, c, at, :] = spread[g * PART : (g + 1) * PART]
                half_out[g, at, :] = spread[(NY + g) * PART : (NY + g + 1) * PART]

        each(0, NZ, unfold)
        half_copy(h).start()
        each(1, NY, lambda d: grad_arrival(h, d).wait_recv())
        grad_keep(h).wait()
        half_arrival(h).wait_recv()

        head = y * NH + h
        own_gain_q = gain_q[pl.ds(head, 1), :]
        own_gain_k = gain_k[pl.ds(head, 1), :]

        def group(g):
            block = packed[h, g].reshape(SLOTS, 3 * HD)
            col = lab_col[g]
            cot = dot(shuffle[...], gob[h, g])
            cot = jnp.where(col > 0.0, cot, 0.0).astype(BF)
            result, term_q, term_k = head_pass(
                block[:, :HD], block[:, HD : 2 * HD], block[:, 2 * HD :], cot,
                own_gain_q, own_gain_k, col, lab_row[g, 0:1, :],
            )
            res[0, g] = result[:HALF]
            res[1, g] = result[HALF:]
            gacc[h, 0:1, :] += term_q
            gacc[h, 1:2, :] += term_k

        each(0, NY, group)
        res_copy(h).start()
        res_copy(h).wait()
        half_copy(h).wait_send()
        z_all(h).wait_send()

    def back_all(b):
        area = zri.at[0, 0 : NZ - 1, :, 0 : 2 * HD]
        return remote(area, area, zrs.at[b], zrr.at[b], mate)

    def send_back(h, half):
        b = h * 2 + half
        part = slice(half * 2 * HD, (half + 1) * 2 * HD)

        def fold(d):
            pz = lax.rem(z + d, NZ)
            at = pl.ds(pl.multiple_of(pz * PART, PART), PART)
            blocks = [res[c, g, at, part] for g in range(NY)] + [rin[g, at, part] for g in range(NY)]
            folded = dot(expand[pz], jnp.concatenate(blocks, axis=0), 0, 0).astype(BF)

            @pl.when(d < NZ)
            def _():
                zro[h, pz, :, part] = folded
                remote(
                    zro.at[h, pz, :, part], zri.at[h, z, :, part], zrs.at[b], zrr.at[b], device(pz, y, c, x)
                ).start()

            @pl.when(d == NZ)
            def _():
                zri[h, z, :, part] = folded

        each(1, NZ + 1, fold)

    def u_own(b):
        h = lax.div(b, 2)
        two = pl.ds(lax.rem(b, 2) * 2, 2)
        return pltpu.make_async_copy(uout.at[h, two, spot], out.at[two, :, columns(y, x, h)], out_own.at[b])

    def u_all(b):
        area = out.at[0:2, :, 0 : (POOL - 1) * HD]
        return remote(area, area, us.at[b], ur.at[b], mate)

    def unpool(h, half):
        b = h * 2 + half
        first = half * 2
        part = slice(first * HD, (first + 2) * HD)
        back_all(b).wait_recv()

        def block(k):
            chosen = turned[pl.ds(pl.multiple_of(k * 4 * ROWS, 4 * ROWS), 4 * ROWS), :]
            found = dot(chosen, zri[h, :, :, part].reshape(NZ * cap, 2 * HD)).astype(BF)
            for r in range(4):
                for m in range(2):
                    uout[h, first + m, k * 4 + r] = found[r * ROWS : (r + 1) * ROWS, m * HD : (m + 1) * HD]

        each(0, POOL // 4, block)

        def start(i):
            py, px = xy_peer(i)
            two = pl.ds(first, 2)
            remote(
                uout.at[h, two, py * NX + px], out.at[two, :, columns(y, x, h)],
                us.at[b], ur.at[b], device(z, py, c, px),
            ).start()

        each(1, POOL, start)
        u_own(b).start()

    def gz_copy(d):
        return remote(gacc, gz.at[z], gzs.at[d], gzr.at[d], device(lax.rem(z + d, NZ), y, c, x))

    def gz_arrival(d):
        pz = lax.rem(z + NZ - d, NZ)
        return remote(gacc, gz.at[pz], gzs.at[d], gzr.at[d], device(pz, y, c, x))

    def gm_copy():
        return remote(gs, gm, gms, gmr, mate)

    def gy_copy(d):
        return remote(gt, gy.at[y], gys.at[d], gyr.at[d], device(z, lax.rem(y + d, NY), c, x))

    def gy_arrival(d):
        py = lax.rem(y + NY - d, NY)
        return remote(gt, gy.at[py], gys.at[d], gyr.at[d], device(z, py, c, x))

    def back(h, half):
        b = h * 2 + half
        if half == 0:

            @pl.when(b < BACKWARD)
            def _():
                work(h)

        @pl.when((b >= BEHIND) & (b < BACKWARD + BEHIND))
        def _():
            back_all(b - BEHIND).wait_send()

        @pl.when(b < BACKWARD)
        def _():
            send_back(h, half)

        @pl.when(b == BACKWARD - 1)
        def _():
            each(1, NZ, lambda d: gz_copy(d).start())
            gz[z] = gacc[...]

        @pl.when(b == BACKWARD)
        def _():
            each(1, NZ, lambda d: gz_arrival(d).wait_recv())
            gs[...] = jnp.sum(gz[...], axis=0)
            gm_copy().start()
            for f in range(3):
                xy_all(0, f, 1).wait_send()
            for h in range(1, NH):
                xy_all(h, 0, 3).wait_send()
            each(0, NH, lambda h: each(1, NY, lambda d: grad_copy(h, d).wait_send()))

        @pl.when(b == BACKWARD + 1)
        def _():
            gm_copy().wait_recv()
            gt[...] = gs[...] + gm[...]
            each(1, NY, lambda d: gy_copy(d).start())
            gy[y] = gt[...]

        @pl.when(b == BACKWARD + 2)
        def _():
            each(1, NY, lambda d: gy_arrival(d).wait_recv())
            gain_out[...] = gy[...]
            each(1, NZ, lambda d: gz_copy(d).wait_send())
            gm_copy().wait_send()
            each(1, NY, lambda d: gy_copy(d).wait_send())

        @pl.when((b >= BEHIND) & (b < BACKWARD + BEHIND))
        def _():
            unpool(h + (half - BEHIND) // 2, (half - BEHIND) % 2)

    def both(h):
        for half in range(2):
            back(h, half)

    each(0, 5, both)

    def finish(b):
        u_all(b).wait()
        u_own(b).wait()

    each(0, BACKWARD, finish)


def exchange(cap, collective_id, *operands):
    vmem = pltpu.VMEM
    dma = pltpu.SemaphoreType.DMA
    any_spec = pl.BlockSpec(memory_space=pl.ANY)
    vmem_spec = pl.BlockSpec(memory_space=pltpu.VMEM)
    scratch = [
        vmem((3, ROWS, FEATURES), BF),
        vmem((SLOTS, 1536), BF),
        vmem((NH, 4, POOL, ROWS, HD), BF),
        vmem((NH, NY, SLOTS, HD), BF),
        vmem((NH, NZ, cap, 3 * HD), BF),
        vmem((NY, HALF, 3 * HD), BF),
        vmem((NH, NY, NC, HALF, 3 * HD), BF),
        vmem((NC, NY, HALF, 4 * HD), BF),
        vmem((NY, HALF, 4 * HD), BF),
        vmem((NH, NZ, cap, 4 * HD), BF),
        vmem((NH, NZ, cap, 4 * HD), BF),
        vmem((NZ * cap, WIDE), BF),
        vmem((WIDE, NZ * cap), BF),
        vmem((NZ, 2 * NY * PART, cap), BF),
        vmem((NY, SLOTS, HD), F32),
        vmem((NY, 8, SLOTS), F32),
        vmem((WIDE, WIDE), BF),
        vmem((SLOTS, SLOTS), BF),
        vmem((NH, 8, HD), F32),
        vmem((NZ, NH, 8, HD), F32),
        vmem((NH, 8, HD), F32),
        vmem((NH, 8, HD), F32),
        vmem((NH, 8, HD), F32),
        vmem((NY, NH, 8, HD), F32),
        dma((4,)),
        dma((OUTWARD,)),
        dma((NH,)),
        dma((BACKWARD,)),
        dma((OUTWARD,)),
        dma((OUTWARD,)),
        dma((NH, NY)),
        dma((NH, NY)),
        dma((NH,)),
        dma((NH, NZ)),
    ]
    scratch += [dma((NH,)), dma((NH,)), dma((NH,)), dma((NH,))]
    scratch += [dma((BACKWARD,)), dma((BACKWARD,)), dma((BACKWARD,)), dma((BACKWARD,))]
    scratch += [dma((NZ,)), dma((NZ,)), dma(()), dma(()), dma((NY,)), dma((NY,))]
    return pl.pallas_call(
        functools.partial(main_kernel, cap),
        name=f"exchange_{cap}",
        out_shape=(
            jax.ShapeDtypeStruct((4, ROWS, FEATURES), BF),
            jax.ShapeDtypeStruct((NY, NH, 8, HD), F32),
        ),
        in_specs=[any_spec] * 4 + [vmem_spec] * 3,
        out_specs=(any_spec, vmem_spec),
        scratch_shapes=scratch,
        compiler_params=pltpu.CompilerParams(
            collective_id=collective_id, has_side_effects=True, vmem_limit_bytes=VMEM_LIMIT
        ),
    )(*operands)


ROOMS = (160, 176, POOL * NY * NC * 2)


def shards(
    query_rows, key_rows, value_rows, destination, image_slot, gain_query, gain_key, grad_output
):
    codes = (destination * 8 + image_slot).reshape(NZ, NY, NC, NX, ROWS)
    codes = codes.transpose(0, 2, 1, 3, 4).reshape(NZ * NC, WIDE)
    operands = (query_rows, key_rows, value_rows, grad_output, gain_query, gain_key, codes)
    planes = codes[:, None, :] >> 6 == jnp.arange(NZ, dtype=jnp.int32)[None, :, None]
    most = jnp.max(jnp.sum(planes.astype(jnp.int32), axis=-1))
    level = sum((most > room).astype(jnp.int32) for room in ROOMS[:-1])
    branches = [functools.partial(exchange, room, k) for k, room in enumerate(ROOMS)]
    out, gains = lax.switch(level, branches, *operands)
    first = lax.axis_index("dp") * 2
    gains = lax.dynamic_slice_in_dim(gains, first, 2, axis=3)
    grad_gain_query = gains[:, :, 0].reshape(NY * NH, 2)
    grad_gain_key = gains[:, :, 1].reshape(NY * NH, 2)
    return (out[0], out[1], out[2], out[3], grad_gain_query, grad_gain_key)


def solution(mesh):
    in_specs = (
        P(("dp", "mp"), None),
        P(("dp", "mp"), None),
        P(("dp", "mp"), None),
        P(),
        P(),
        P("mp", None),
        P("mp", None),
        P("dp", "mp"),
    )
    out_specs = (
        P(("dp", "mp"), None),
        P(("dp", "mp"), None),
        P(("dp", "mp"), None),
        P(("dp", "mp"), None),
        P("mp", "dp"),
        P("mp", "dp"),
    )
    return jax.shard_map(shards, mesh=mesh, in_specs=in_specs, out_specs=out_specs, check_vma=False)
```
